512 devices in a mesh: grp: 16 (over x_lo, y), dom: 32 (over x_hi, z, core).
Axes of the slice: x: 4 (x_hi: 2, x_lo: 2; x = x_hi * 2 + x_lo), y: 8, z: 8, core: 2. Of those that a mesh axis runs over, the one named last changes fastest.
Arguments:
- pair_blocks: bfloat16 [16, 4096, 3, 4096], P('grp', 'dom'), may hold values from -3 to 3
- pair_target: int32 [16, 4096], P('grp', 'dom'), may hold values from 0 to 31, as said below
- ghost_source: int32 [16, 32, 2, 8], P('grp', 'dom'), may hold values from 0 to 15, as said below
- weight_code: int32 [16, 512], P('grp', 'dom'), may hold values from 0 to 3
- ref_forces: float32 [16, 512, 3], P('grp', 'dom'), may hold values from -6 to 6
Outputs:
- gram: float32 [4096, 4096], P('grp', 'dom')
- rhs: float32 [4096], P('dom')
The draws below stay inside these ranges and needn't reach their ends.
Inputs may be any that keep to these rules, and one draw needn't show every extreme that they name: `pair_target`: A pair's neighbour slot is never its centre atom. `ghost_source`: entries are distinct within each snapshot, domain and side.
All inputs are finite; a program needn't handle non-finite values.
Results may differ from the reference program's by a relative error of at most 0.0041.
Values may be sent and summed in bfloat16 or wider, within the bound.
A program may use at most 64 MiB of HBM per device.

```python
import jax
import jax.numpy as jnp
from jax import lax

K = 4096
ATOMS = 16
NBR = 8
GHOSTS = 8
PAIRS = 128
SLOTS = 32
ROWS_ALL = 24576
N_GRP = 16
N_DOM = 32


def draw_pair_target(key, part):
    key = jax.random.fold_in(key, 11)
    slot_count = ATOMS + 2 * GHOSTS
    offsets = jax.random.randint(key, (N_GRP, N_DOM * PAIRS), 0, slot_count - 1)
    center = jnp.arange(N_DOM * PAIRS) % PAIRS // NBR
    return ((center[None, :] + 1 + offsets) % slot_count).astype(jnp.int32)


def draw_ghost_source(key, part):
    key = jax.random.fold_in(key, 23)
    scores = jax.random.randint(key, (N_GRP, N_DOM, 2, ATOMS), 0, 1048576) * ATOMS + jnp.arange(ATOMS)
    ranking = jnp.argsort(scores, axis=-1)
    return ranking[..., :GHOSTS].astype(jnp.int32)


def place_ends(entries, own_key, low, high):
    spot = [jax.random.randint(jax.random.fold_in(own_key, axis), (), 0, length) for axis, length in enumerate(entries.shape)]
    main_axis = entries.shape.index(max(entries.shape))
    next_to = spot[:main_axis] + [(spot[main_axis] + 1) % entries.shape[main_axis]] + spot[main_axis + 1:]
    return entries.at[tuple(spot)].set(low).at[tuple(next_to)].set(high)


def shard_levels(own_key, extent, shards, low, largest):
    gain = 1.0
    for axis_at, shards_of in shards:
        heights = jax.random.uniform(jax.random.fold_in(jax.random.fold_in(own_key, 6), axis_at), (shards_of,), jnp.float32, low / len(shards), largest / len(shards))
        gain = gain * jnp.repeat(jnp.exp(heights), extent[axis_at] // shards_of).reshape((-1,) + (1,) * (len(extent) - 1 - axis_at))
    return gain


def noise(rng, extent, spread, limit, cuts=(), dtype=jnp.bfloat16):
    loudness = shard_levels(rng, extent, cuts, -0.22, 0.18) if cuts else 1.0
    entries = jax.random.normal(rng, extent, jnp.float32) * spread * loudness
    return jnp.minimum(jnp.maximum(entries, -limit), limit).astype(dtype)


def setup_inputs(seed: int = 0) -> dict:
    keys = jax.random.split(jax.random.key(seed), 6)
    return {
        "pair_blocks": noise(keys[0], (N_GRP, N_DOM * PAIRS, 3, K), 0.35, 3.0, ((0, 16), (1, 32))),
        "pair_target": draw_pair_target(jax.random.fold_in(keys[5], 71), 0),
        "ghost_source": draw_ghost_source(jax.random.fold_in(keys[5], 71), 0),
        "weight_code": place_ends(jax.random.randint(keys[3], (N_GRP, N_DOM * ATOMS), 0, 4), jax.random.fold_in(keys[3], 1), 0, 3).astype(jnp.int32),
        "ref_forces": noise(keys[4], (N_GRP, N_DOM * ATOMS, 3), 1.0, 6.0, ((0, 16), (1, 32)), jnp.float32),
    }


def reference(pair_blocks, pair_target, ghost_source, weight_code, ref_forces):
    pair_index = jnp.arange(N_DOM * PAIRS)
    domain_of = (pair_index // PAIRS).astype(jnp.int32)
    center = (pair_index % PAIRS // NBR).astype(jnp.int32)
    domain_ids = jnp.arange(N_DOM)[:, None]

    def group_step(totals, inputs):
        blocks, target, sources, codes, forces = inputs
        blocks = blocks.astype(jnp.float32)
        slot_rows = jnp.zeros((N_DOM * SLOTS, 3, K), jnp.float32)
        slot_rows = slot_rows.at[domain_of * SLOTS + center].add(blocks)
        slot_rows = slot_rows.at[domain_of * SLOTS + target].add(-blocks)
        slot_rows = slot_rows.reshape(N_DOM, SLOTS, 3, K)
        owned_rows = slot_rows[:, :ATOMS]
        lower_rows = slot_rows[:, ATOMS:ATOMS + GHOSTS]
        upper_rows = slot_rows[:, ATOMS + GHOSTS:]
        from_upper = jnp.roll(lower_rows, -1, 0)
        from_lower = jnp.roll(upper_rows, 1, 0)
        owned_rows = owned_rows.at[domain_ids, sources[:, 0]].add(from_upper)
        owned_rows = owned_rows.at[domain_ids, sources[:, 1]].add(from_lower)
        row_scale = (1.0 + codes.astype(jnp.float32)) * 0.5
        design = (owned_rows.reshape(N_DOM * ATOMS, 3, K) * row_scale[:, None, None]).astype(jnp.bfloat16)
        design = design.reshape(N_DOM * ATOMS * 3, K)
        targets = (forces * row_scale[:, None]).astype(jnp.bfloat16).reshape(N_DOM * ATOMS * 3)
        gram_sum = totals[0] + jnp.dot(design.T, design, preferred_element_type=jnp.float32)
        rhs_sum = totals[1] + jnp.dot(targets, design, preferred_element_type=jnp.float32)
        return ((gram_sum, rhs_sum), None)
    start = (jnp.zeros((K, K), jnp.float32), jnp.zeros((K,), jnp.float32))
    totals, _ = lax.scan(group_step, start, (pair_blocks, pair_target, ghost_source, weight_code, ref_forces))
    factor = 1.0 / jnp.sqrt(jnp.float32(ROWS_ALL))
    return (totals[0] * factor, totals[1] * factor)
```

```python
import functools
import math

import jax
import jax.numpy as jnp
from jax import lax
from jax.experimental import pallas as pl
from jax.experimental.pallas import tpu as pltpu
from jax.sharding import PartitionSpec as P

MESH = pl.DeviceIdType.MESH
RING = 8
XS = 4
BLOCKS = 5
CHUNKS = 4
F32 = jnp.float32
BF16 = jnp.bfloat16


def chain_lengths(k):
    return (4, 3) if k % 2 == 0 else (3, 4)


def kernel(
    blocks,
    target_ref,
    ghost_ref,
    weight_ref,
    force_ref,
    gram_ref,
    rhs_ref,
    pairs,
    own,
    ghost_out,
    ghost_in,
    rows,
    partial,
    ring_out,
    ring_in,
    kept,
    second_out,
    second_in,
    mirror_out,
    mirror_in,
    rhs_part,
    rhs_in_z,
    rhs_mid,
    rhs_in_y,
    load_sem,
    ghost_send,
    ghost_recv,
    x_send,
    x_recv,
    ring_send,
    ring_recv,
    second_send,
    second_recv,
    mirror_send,
    mirror_recv,
    rhs_send,
    rhs_recv,
):
    basis = blocks.shape[2]
    pair_count = blocks.shape[1]
    atoms = weight_ref.shape[1]
    half_basis = basis // 2
    width = basis // CHUNKS
    half_width = width // 2

    g = lax.axis_index("grp")
    d = lax.axis_index("dom")
    xl, y = g // RING, g % RING
    xh, z, core = d // (2 * RING), (d // 2) % RING, d % 2
    x = xh * 2 + xl
    delta = (z - y + RING) % RING

    def device(x_, y_, z_, core_):
        return {
            "grp": (x_ % 2) * RING + y_,
            "dom": (x_ // 2) * (2 * RING) + z_ * 2 + core_,
        }

    sibling = device(x, y, z, 1 - core)
    right = device((x + 1) % XS, y, z, core)
    left = device((x + XS - 1) % XS, y, z, core)
    dom_count = 4 * RING
    below = {"grp": g, "dom": (d + dom_count - 1) % dom_count}
    above = {"grp": g, "dom": (d + 1) % dom_count}
    off_chip = {"grp": g, "dom": (d + dom_count - 1 + 2 * core) % dom_count}
    mirror_x = (x % 2) * 2 + x // 2

    def remote(src, dst, send_sem, recv_sem, to):
        return pltpu.make_async_remote_copy(
            src_ref=src,
            dst_ref=dst,
            send_sem=send_sem,
            recv_sem=recv_sem,
            device_id=to,
            device_id_type=MESH,
        )

    def load(q):
        columns = pl.ds(q * width, width)
        return pltpu.make_async_copy(
            blocks.at[:, :, columns], pairs.at[:, :, columns], load_sem.at[q]
        )

    for q in range(CHUNKS):
        load(q).start()

    barrier = pltpu.get_barrier_semaphore()

    def greet(to):
        pl.semaphore_signal(barrier, inc=1, device_id=to, device_id_type=MESH)

    for to in (sibling, right, left, off_chip):
        greet(to)
    for step in range(1, RING):
        greet(device(x, (y + step) % RING, z, core))
        greet(device(x, y, (z + step) % RING, core))

    @pl.when(delta % 4 != 0)
    def _():
        greet(device(mirror_x, z, y, 0))
        greet(device(mirror_x, z, y, 1))

    slots = 2 * atoms
    per_atom = pair_count // atoms
    slot_ids = lax.broadcasted_iota(jnp.int32, (slots, pair_count), 0)
    pair_ids = lax.broadcasted_iota(jnp.int32, (slots, pair_count), 1)
    center = pair_ids // per_atom
    signs = (
        (slot_ids == center).astype(F32) - (slot_ids == target_ref[...]).astype(F32)
    ).astype(BF16)

    ghosts = atoms // 2
    row_ids = lax.broadcasted_iota(jnp.int32, (2 * atoms, 2 * atoms), 0)
    col_ids = lax.broadcasted_iota(jnp.int32, (2 * atoms, 2 * atoms), 1)
    source = jnp.zeros((2 * atoms, 2 * atoms), jnp.int32)
    for side in range(2):
        for ghost in range(ghosts):
            here = (col_ids // atoms == side) & (col_ids % ghosts == ghost)
            source = jnp.where(here, ghost_ref[side, ghost], source)
    placed = (row_ids % atoms == source) & (
        row_ids // atoms == (col_ids // ghosts) % 2
    )
    placed = placed.astype(F32).astype(BF16)

    diagonal = lax.broadcasted_iota(jnp.int32, (atoms, atoms), 0) == (
        lax.broadcasted_iota(jnp.int32, (atoms, atoms), 1)
    )

    def as_column(row):
        return jnp.sum(jnp.where(diagonal, row, 0.0), axis=1, keepdims=True)

    scale = as_column((1.0 + weight_ref[...].astype(F32)) * 0.5)
    first_lane = lax.broadcasted_iota(jnp.int32, (atoms, 128), 1) == 0
    my_slot = x * 2 + core
    for comp in range(3):
        column = as_column(force_ref[comp]) * scale
        rows[my_slot, comp * atoms : (comp + 1) * atoms, basis:] = jnp.where(
            first_lane, column, 0.0
        ).astype(BF16)

    def ghost_copy(side, q):
        return remote(
            ghost_out.at[q, side],
            ghost_in.at[q, pl.ds(side * 16, 16)],
            ghost_send.at[side, q],
            ghost_recv.at[side, q],
            below if side == 0 else above,
        )

    for q in range(CHUNKS):
        load(q).wait()
        columns = pl.ds(q * width, width)
        ghost_rows = []
        for comp in range(3):
            slot_rows = jnp.dot(signs, pairs[comp, :, columns], preferred_element_type=F32)
            own[comp, :, columns] = slot_rows[:atoms]
            ghost_rows.append(slot_rows[atoms:])
        for side in range(2):
            part = [rows_[side * ghosts : (side + 1) * ghosts] for rows_ in ghost_rows]
            ghost_out[q, side, :, :width] = jnp.concatenate(part[:2], axis=0).astype(BF16)
            ghost_out[q, side, :, width:] = jnp.concatenate(
                [part[2][:, :half_width], part[2][:, half_width:]], axis=0
            ).astype(BF16)
        if q == 0:
            extra = 2 * (delta % 4 != 0).astype(jnp.int32)
            pl.semaphore_wait(barrier, 4 + 2 * (RING - 1) + extra)
        for side in range(2):
            ghost_copy(side, q).start()

    def span(q, part):
        start, stop = q * width, (q + 1) * width
        middle = start + half_width
        if q == CHUNKS - 1:
            stop = stop + 128
        if part == 0:
            stop = middle
        elif part == 1:
            start = middle
        return pl.ds(start, stop - start)

    slot_right = ((x + 1) % XS) * 2
    slot_left = ((x + XS - 1) % XS) * 2
    slot_far = ((x + 2) % XS) * 2

    def x_copy(kind, q):
        slot, part, to = (
            (my_slot, None, sibling),
            (my_slot, None, right),
            (my_slot, None, left),
            (slot_left + core, None, sibling),
            (slot_right + core, None, sibling),
            (slot_left + core, 0, right),
            (slot_right + core, 1, left),
            (slot_far + core, 0, sibling),
            (slot_far + core, 1, sibling),
        )[kind]
        piece = rows.at[slot, :, span(q, part)]
        return remote(piece, piece, x_send.at[kind, q], x_recv.at[kind, q], to)

    for q in range(CHUNKS):
        columns = pl.ds(q * width, width)
        for side in range(2):
            ghost_copy(side, q).wait_recv()
        placed_rows = jnp.dot(placed, ghost_in[q], preferred_element_type=F32)
        for comp in range(3):
            if comp < 2:
                added = placed_rows[comp * atoms : (comp + 1) * atoms, :width]
            else:
                added = jnp.concatenate(
                    [placed_rows[:atoms, width:], placed_rows[atoms:, width:]], axis=1
                )
            rows[my_slot, comp * atoms : (comp + 1) * atoms, columns] = (
                (own[comp, :, columns] + added) * scale
            ).astype(BF16)
        for kind in (1, 2, 0):
            x_copy(kind, q).start()

    for q in range(CHUNKS):
        for kind, relays in ((1, (5, 3)), (2, (6, 4))):
            x_copy(kind, q).wait_recv()
            for relay in relays:
                x_copy(relay, q).start()
    for q in range(CHUNKS):
        for kind, relay in ((5, 7), (6, 8)):
            x_copy(kind, q).wait_recv()
            x_copy(relay, q).start()
    for q in range(CHUNKS):
        for kind in (0, 3, 4, 7, 8):
            x_copy(kind, q).wait_recv()

    contract = (((0,), (0,)), ((), ()))
    depth = rows.shape[0] * rows.shape[1]

    def right_block(c):
        start = pl.multiple_of(xh * half_basis + (2 * c + core) * 128, 128)
        return rows[:, :, pl.ds(start, 128)].reshape(depth, 128)

    target_rows = rows[:, :, basis:].reshape(depth, 128)
    for c in range(RING):
        rhs_part[c] = lax.dot_general(
            target_rows, right_block(c), contract, preferred_element_type=F32
        )[:8]

    def rhs_copy_z(step):
        to_z = (z + step) % RING
        return remote(
            rhs_part.at[to_z],
            rhs_in_z.at[step - 1],
            rhs_send.at[0, step - 1],
            rhs_recv.at[0, step - 1],
            device(x, y, to_z, core),
        )

    for step in range(1, RING):
        rhs_copy_z(step).start()

    def product(r, carry):
        start = pl.multiple_of(xl * half_basis + r * 256, 256)
        left_block = rows[:, :, pl.ds(start, 256)].reshape(depth, 256)
        right_blocks = jnp.concatenate(
            [right_block((r + k) % RING) for k in range(BLOCKS)], axis=1
        )
        tile = lax.dot_general(
            left_block, right_blocks, contract, preferred_element_type=F32
        )
        for k in range(BLOCKS):
            columns = slice(k * 128, (k + 1) * 128)
            partial[0, r, k] = tile[:128, columns]
            partial[1, (r + k) % RING, k] = tile[128:, columns]
        return carry

    lax.fori_loop(0, RING, product, 0)

    def ring_copy(h, way, step, k):
        if step == 0:
            src = ring_out.at[h, way, k]
        else:
            src = ring_in.at[h, way, step - 1, k]
        by = 1 if way == 0 else RING - 1
        if h == 0:
            to = device(x, (y + by) % RING, z, core)
        else:
            to = device(x, y, (z + by) % RING, core)
        return remote(
            src,
            ring_in.at[h, way, step, k],
            ring_send.at[h, way, step, k],
            ring_recv.at[h, way, step, k],
            to,
        )

    for step in range(4):
        for k in range(BLOCKS):
            for h in range(2):
                here = y if h == 0 else z
                for way in range(2):
                    length = chain_lengths(k)[way]
                    if step >= length:
                        continue
                    if way == 0:
                        dest = (here + length - step) % RING
                    else:
                        dest = (here + RING - length + step) % RING
                    term = partial[h, dest, k]
                    if step == 0:
                        ring_out[h, way, k] = term.astype(BF16)
                    else:
                        ring_copy(h, way, step - 1, k).wait_recv()
                        ring_in[h, way, step - 1, k] = (
                            ring_in[h, way, step - 1, k].astype(F32) + term
                        ).astype(BF16)
                    ring_copy(h, way, step, k).start()
        if step == 0:
            total = rhs_part[z]
            for back in range(1, RING):
                rhs_copy_z(back).wait_recv()
                total = total + rhs_in_z[back - 1]
            rhs_mid[...] = total

            def rhs_copy_y(step_):
                return remote(
                    rhs_mid,
                    rhs_in_y.at[step_ - 1],
                    rhs_send.at[1, step_ - 1],
                    rhs_recv.at[1, step_ - 1],
                    device(x, (y + step_) % RING, z, core),
                )

            for step_ in range(1, RING):
                rhs_copy_y(step_).start()

    def second_copy(h, k):
        if h == 0:
            offset = (y + k + RING - z) % RING
            to = device(x, y, (y + k) % RING, core)
        else:
            offset = (z + RING - k + RING - y) % RING
            to = device(x, (z + RING - k) % RING, z, core)
        return remote(
            second_out.at[h, k],
            second_in.at[h, offset],
            second_send.at[h, k],
            second_recv.at[h, offset],
            to,
        )

    for k in range(BLOCKS):
        for h in range(2):
            here = y if h == 0 else z
            total = partial[h, here, k]
            for way in range(2):
                length = chain_lengths(k)[way]
                ring_copy(h, way, length - 1, k).wait_recv()
                total = total + ring_in[h, way, length - 1, k].astype(F32)

            @pl.when(delta == k)
            def _():
                kept[h] = total

            @pl.when(delta != k)
            def _():
                second_out[h, k] = total.astype(BF16)
                second_copy(h, k).start()

    total = rhs_mid[...]
    for step in range(1, RING):
        rhs_copy_y(step).wait_recv()
        total = total + rhs_in_y[step - 1]
    rhs_ref[...] = total[:1]

    def mirror_copy(h):
        return remote(
            mirror_out.at[h],
            mirror_in.at[core],
            mirror_send.at[h],
            mirror_recv.at[core],
            device(mirror_x, z, y, h),
        )

    def second_arrival(h, offset):
        return remote(
            second_out.at[h, 0],
            second_in.at[h, offset],
            second_send.at[h, 0],
            second_recv.at[h, offset],
            sibling,
        )

    @pl.when(delta < BLOCKS)
    def _():
        for h in range(2):
            total = kept[h]
            for offset in range(1, RING):
                second_arrival(h, offset).wait_recv()
                total = total + second_in[h, offset].astype(F32)
            gram_ref[h * 128 : (h + 1) * 128, :] = total
            mirror_out[h] = total.T

            @pl.when((delta > 0) & (delta < 4))
            def _():
                mirror_copy(h).start()

    @pl.when(delta >= BLOCKS)
    def _():
        for sender in range(2):
            remote(
                mirror_out.at[0],
                mirror_in.at[sender],
                mirror_send.at[0],
                mirror_recv.at[sender],
                sibling,
            ).wait_recv()
            gram_ref[sender * 128 : (sender + 1) * 128, :] = mirror_in[sender]

    for q in range(CHUNKS):
        for side in range(2):
            ghost_copy(side, q).wait_send()
        for kind in range(9):
            x_copy(kind, q).wait_send()
    for k in range(BLOCKS):
        for h in range(2):
            for way in range(2):
                for step in range(chain_lengths(k)[way]):
                    ring_copy(h, way, step, k).wait_send()

            @pl.when(delta != k)
            def _():
                second_copy(h, k).wait_send()

    for step in range(1, RING):
        rhs_copy_z(step).wait_send()
        rhs_copy_y(step).wait_send()

    @pl.when((delta > 0) & (delta < 4))
    def _():
        for h in range(2):
            mirror_copy(h).wait_send()


def per_device(pair_blocks, pair_target, ghost_source, weight_code, ref_forces):
    _, pair_count, comps, basis = pair_blocks.shape
    atoms = weight_code.shape[1]
    width = basis // CHUNKS
    dom_count = lax.axis_size("dom")
    grp_count = lax.axis_size("grp")
    factor = 1.0 / math.sqrt(comps * atoms * dom_count * grp_count)
    dma = pltpu.SemaphoreType.DMA
    vmem = pl.BlockSpec(memory_space=pltpu.VMEM)
    gram, rhs = pl.pallas_call(
        kernel,
        out_shape=(
            jax.ShapeDtypeStruct((256, 128), F32),
            jax.ShapeDtypeStruct((1, 128), F32),
        ),
        in_specs=[
            pl.BlockSpec(memory_space=pl.ANY),
            vmem,
            pl.BlockSpec(memory_space=pltpu.SMEM),
            vmem,
            vmem,
        ],
        out_specs=(vmem, vmem),
        scratch_shapes=[
            pltpu.VMEM((comps, pair_count, basis), BF16),
            pltpu.VMEM((comps, atoms, basis), F32),
            pltpu.VMEM((CHUNKS, 2, 16, width * 3 // 2), BF16),
            pltpu.VMEM((CHUNKS, 32, width * 3 // 2), BF16),
            pltpu.VMEM((2 * XS, comps * atoms, basis + 128), BF16),
            pltpu.VMEM((2, RING, BLOCKS, 128, 128), F32),
            pltpu.VMEM((2, 2, BLOCKS, 128, 128), BF16),
            pltpu.VMEM((2, 2, 4, BLOCKS, 128, 128), BF16),
            pltpu.VMEM((2, 128, 128), F32),
            pltpu.VMEM((2, BLOCKS, 128, 128), BF16),
            pltpu.VMEM((2, RING, 128, 128), BF16),
            pltpu.VMEM((2, 128, 128), F32),
            pltpu.VMEM((2, 128, 128), F32),
            pltpu.VMEM((RING, 8, 128), F32),
            pltpu.VMEM((RING - 1, 8, 128), F32),
            pltpu.VMEM((8, 128), F32),
            pltpu.VMEM((RING - 1, 8, 128), F32),
            dma((CHUNKS,)),
            dma((2, CHUNKS)),
            dma((2, CHUNKS)),
            dma((9, CHUNKS)),
            dma((9, CHUNKS)),
            dma((2, 2, 4, BLOCKS)),
            dma((2, 2, 4, BLOCKS)),
            dma((2, BLOCKS)),
            dma((2, RING)),
            dma((2,)),
            dma((2,)),
            dma((2, RING - 1)),
            dma((2, RING - 1)),
        ],
        compiler_params=pltpu.CompilerParams(
            collective_id=0,
            has_side_effects=True,
            vmem_limit_bytes=48 * 1024 * 1024,
        ),
    )(
        jnp.transpose(pair_blocks[0], (1, 0, 2)),
        pair_target,
        ghost_source[0, 0],
        weight_code,
        jnp.transpose(ref_forces, (2, 0, 1)),
    )
    return gram * factor, rhs.reshape(128) * factor


def solution(mesh):
    return jax.shard_map(
        per_device,
        mesh=mesh,
        in_specs=(
            P("grp", "dom", None, None),
            P("grp", "dom"),
            P("grp", "dom", None, None),
            P("grp", "dom"),
            P("grp", "dom", None),
        ),
        out_specs=(P("grp", "dom"), P("dom")),
        check_vma=False,
    )
```

```python
import functools
import math

import jax
import jax.numpy as jnp
from jax import lax
from jax.experimental import pallas as pl
from jax.experimental.pallas import tpu as pltpu
from jax.sharding import PartitionSpec as P

MESH = pl.DeviceIdType.MESH
RING = 8
XS = 4
OFFSETS = (1, 3, 6, 0, 4)
BLOCKS = len(OFFSETS)
CHUNKS = 4
F32 = jnp.float32
BF16 = jnp.bfloat16


def chain_lengths(k):
    return (4, 3) if k % 2 == 0 else (3, 4)


def kernel(
    blocks,
    target_hbm,
    ghost_hbm,
    weight_hbm,
    force_hbm,
    gram_ref,
    rhs_ref,
    target_ref,
    ghost_ref,
    weight_ref,
    force_ref,
    pairs,
    own,
    ghost_out,
    ghost_in,
    rows,
    partial,
    ring_out,
    ring_in,
    kept,
    second_out,
    second_in,
    mirror_out,
    mirror_in,
    rhs_part,
    rhs_in_z,
    rhs_mid,
    rhs_in_y,
    load_sem,
    small_sem,
    ghost_send,
    ghost_recv,
    x_send,
    x_recv,
    ring_send,
    ring_recv,
    second_send,
    second_recv,
    mirror_send,
    mirror_recv,
    rhs_send,
    rhs_recv,
):
    basis = blocks.shape[2]
    pair_count = blocks.shape[1]
    atoms = weight_ref.shape[1]
    half_basis = basis // 2
    width = basis // CHUNKS
    half_width = width // 2

    g = lax.axis_index("grp")
    d = lax.axis_index("dom")
    xl, y = g // RING, g % RING
    xh, z, core = d // (2 * RING), (d // 2) % RING, d % 2
    x = xh * 2 + xl
    delta = (z - y + RING) % RING

    def device(x_, y_, z_, core_):
        return {
            "grp": (x_ % 2) * RING + y_,
            "dom": (x_ // 2) * (2 * RING) + z_ * 2 + core_,
        }

    sibling = device(x, y, z, 1 - core)
    right = device((x + 1) % XS, y, z, core)
    left = device((x + XS - 1) % XS, y, z, core)
    dom_count = 4 * RING
    below = {"grp": g, "dom": (d + dom_count - 1) % dom_count}
    above = {"grp": g, "dom": (d + 1) % dom_count}
    off_chip = {"grp": g, "dom": (d + dom_count - 1 + 2 * core) % dom_count}
    mirror_x = (x % 2) * 2 + x // 2

    def remote(src, dst, send_sem, recv_sem, to):
        return pltpu.make_async_remote_copy(
            src_ref=src,
            dst_ref=dst,
            send_sem=send_sem,
            recv_sem=recv_sem,
            device_id=to,
            device_id_type=MESH,
        )

    def load(q):
        columns = pl.ds(q * width, width)
        return pltpu.make_async_copy(
            blocks.at[:, :, columns], pairs.at[:, :, columns], load_sem.at[q]
        )

    small_loads = [
        pltpu.make_async_copy(source, place, small_sem.at[i])
        for i, (source, place) in enumerate(
            (
                (target_hbm, target_ref),
                (ghost_hbm, ghost_ref),
                (weight_hbm, weight_ref),
                (force_hbm, force_ref),
            )
        )
    ]
    for copy in small_loads:
        copy.start()
    for q in range(CHUNKS):
        load(q).start()

    barrier = pltpu.get_barrier_semaphore()

    def greet(to):
        pl.semaphore_signal(barrier, inc=1, device_id=to, device_id_type=MESH)

    for to in (sibling, right, left, off_chip):
        greet(to)
    for step in range(1, RING):
        greet(device(x, (y + step) % RING, z, core))
        greet(device(x, y, (z + step) % RING, core))

    sends_mirror = (delta == OFFSETS[0]) | (delta == OFFSETS[1]) | (delta == OFFSETS[2])
    takes_mirror = jnp.logical_not(sends_mirror) & (delta % 4 != 0)

    @pl.when(delta % 4 != 0)
    def _():
        greet(device(mirror_x, z, y, 0))
        greet(device(mirror_x, z, y, 1))

    for copy in small_loads:
        copy.wait()

    slots = 2 * atoms
    per_atom = pair_count // atoms
    slot_ids = lax.broadcasted_iota(jnp.int32, (slots, pair_count), 0)
    pair_ids = lax.broadcasted_iota(jnp.int32, (slots, pair_count), 1)
    center = pair_ids // per_atom
    signs = (
        (slot_ids == center).astype(F32) - (slot_ids == target_ref[...]).astype(F32)
    ).astype(BF16)

    ghosts = atoms // 2
    row_ids = lax.broadcasted_iota(jnp.int32, (2 * atoms, 2 * atoms), 0)
    col_ids = lax.broadcasted_iota(jnp.int32, (2 * atoms, 2 * atoms), 1)
    source = jnp.zeros((2 * atoms, 2 * atoms), jnp.int32)
    for side in range(2):
        for ghost in range(ghosts):
            here = (col_ids // atoms == side) & (col_ids % ghosts == ghost)
            source = jnp.where(here, ghost_ref[side, ghost], source)
    placed = (row_ids % atoms == source) & (
        row_ids // atoms == (col_ids // ghosts) % 2
    )
    placed = placed.astype(F32).astype(BF16)

    diagonal = lax.broadcasted_iota(jnp.int32, (atoms, atoms), 0) == (
        lax.broadcasted_iota(jnp.int32, (atoms, atoms), 1)
    )

    def as_column(row):
        return jnp.sum(jnp.where(diagonal, row, 0.0), axis=1, keepdims=True)

    scale = as_column((1.0 + weight_ref[...].astype(F32)) * 0.5)
    first_lane = lax.broadcasted_iota(jnp.int32, (atoms, 128), 1) == 0
    my_slot = x * 2 + core
    for comp in range(3):
        column = as_column(force_ref[comp]) * scale
        rows[my_slot, comp * atoms : (comp + 1) * atoms, basis:] = jnp.where(
            first_lane, column, 0.0
        ).astype(BF16)

    def ghost_copy(side, q):
        return remote(
            ghost_out.at[q, side],
            ghost_in.at[q, pl.ds(side * 16, 16)],
            ghost_send.at[side, q],
            ghost_recv.at[side, q],
            below if side == 0 else above,
        )

    def slots_of(q):
        load(q).wait()
        columns = pl.ds(q * width, width)
        ghost_rows = []
        for comp in range(3):
            slot_rows = jnp.dot(signs, pairs[comp, :, columns], preferred_element_type=F32)
            own[comp, :, columns] = slot_rows[:atoms]
            ghost_rows.append(slot_rows[atoms:])
        for side in range(2):
            part = [rows_[side * ghosts : (side + 1) * ghosts] for rows_ in ghost_rows]
            ghost_out[q, side, :, :width] = jnp.concatenate(part[:2], axis=0).astype(BF16)
            ghost_out[q, side, :, width:] = jnp.concatenate(
                [part[2][:, :half_width], part[2][:, half_width:]], axis=0
            ).astype(BF16)
        if q == 0:
            extra = 2 * (delta % 4 != 0).astype(jnp.int32)
            pl.semaphore_wait(barrier, 4 + 2 * (RING - 1) + extra)
        for side in range(2):
            ghost_copy(side, q).start()

    def span(q, part):
        start, stop = q * width, (q + 1) * width
        middle = start + half_width
        if q == CHUNKS - 1:
            stop = stop + 128
        if part == 0:
            stop = middle
        elif part == 1:
            start = middle
        return pl.ds(start, stop - start)

    slot_right = ((x + 1) % XS) * 2
    slot_left = ((x + XS - 1) % XS) * 2
    slot_far = ((x + 2) % XS) * 2

    def x_copy(kind, q):
        slot, part, to = (
            (my_slot, None, sibling),
            (my_slot, None, right),
            (my_slot, None, left),
            (slot_left + core, None, sibling),
            (slot_right + core, None, sibling),
            (slot_left + core, 0, right),
            (slot_right + core, 1, left),
            (slot_far + core, 0, sibling),
            (slot_far + core, 1, sibling),
        )[kind]
        piece = rows.at[slot, :, span(q, part)]
        return remote(piece, piece, x_send.at[kind, q], x_recv.at[kind, q], to)

    def design_of(q):
        columns = pl.ds(q * width, width)
        for side in range(2):
            ghost_copy(side, q).wait_recv()
        placed_rows = jnp.dot(placed, ghost_in[q], preferred_element_type=F32)
        for comp in range(3):
            if comp < 2:
                added = placed_rows[comp * atoms : (comp + 1) * atoms, :width]
            else:
                added = jnp.concatenate(
                    [placed_rows[:atoms, width:], placed_rows[atoms:, width:]], axis=1
                )
            rows[my_slot, comp * atoms : (comp + 1) * atoms, columns] = (
                (own[comp, :, columns] + added) * scale
            ).astype(BF16)
        for kind in (1, 2, 0):
            x_copy(kind, q).start()

    slots_of(0)
    for q in range(1, CHUNKS):
        slots_of(q)
        design_of(q - 1)
    design_of(CHUNKS - 1)

    for q in range(CHUNKS):
        for kind, relays in ((1, (5, 3)), (2, (6, 4))):
            x_copy(kind, q).wait_recv()
            for relay in relays:
                x_copy(relay, q).start()
    for q in range(CHUNKS):
        for kind, relay in ((5, 7), (6, 8)):
            x_copy(kind, q).wait_recv()
            x_copy(relay, q).start()
    for q in range(CHUNKS):
        for kind in (0, 3, 4, 7, 8):
            x_copy(kind, q).wait_recv()

    contract = (((0,), (0,)), ((), ()))
    depth = rows.shape[0] * rows.shape[1]

    def right_block(c):
        start = pl.multiple_of(xh * half_basis + (2 * c + core) * 128, 128)
        return rows[:, :, pl.ds(start, 128)].reshape(depth, 128)

    def left_block(h, r):
        start = pl.multiple_of(xl * half_basis + (2 * r + h) * 128, 128)
        return rows[:, :, pl.ds(start, 128)].reshape(depth, 128)

    def product(by):
        r = (y + by + RING) % RING
        right_blocks = jnp.concatenate(
            [right_block((r + offset) % RING) for offset in OFFSETS], axis=1
        )
        tile = lax.dot_general(
            left_block(0, r), right_blocks, contract, preferred_element_type=F32
        )
        for k in range(BLOCKS):
            partial[0, r, k] = tile[:, k * 128 : (k + 1) * 128]
        c = (z + by + RING) % RING
        left_blocks = jnp.concatenate(
            [left_block(1, (c + RING - offset) % RING) for offset in OFFSETS], axis=1
        )
        tile = lax.dot_general(
            left_blocks, right_block(c), contract, preferred_element_type=F32
        )
        for k in range(BLOCKS):
            partial[1, c, k] = tile[k * 128 : (k + 1) * 128]

    def rhs_copy_z(step):
        to_z = (z + step) % RING
        return remote(
            rhs_part.at[to_z],
            rhs_in_z.at[step - 1],
            rhs_send.at[0, step - 1],
            rhs_recv.at[0, step - 1],
            device(x, y, to_z, core),
        )

    def rhs_copy_y(step):
        return remote(
            rhs_mid,
            rhs_in_y.at[step - 1],
            rhs_send.at[1, step - 1],
            rhs_recv.at[1, step - 1],
            device(x, (y + step) % RING, z, core),
        )

    def ring_copy(h, way, step, k):
        if step == 0:
            src = ring_out.at[h, way, k]
        else:
            src = ring_in.at[h, way, step - 1, k]
        by = 1 if way == 0 else RING - 1
        if h == 0:
            to = device(x, (y + by) % RING, z, core)
        else:
            to = device(x, y, (z + by) % RING, core)
        return remote(
            src,
            ring_in.at[h, way, step, k],
            ring_send.at[h, way, step, k],
            ring_recv.at[h, way, step, k],
            to,
        )

    for step, ahead in enumerate(((4, 3, -3), (2, -2), (1, -1), (0,))):
        for by in ahead:
            product(by)
        for k in range(BLOCKS):
            for h in range(2):
                here = y if h == 0 else z
                for way in range(2):
                    length = chain_lengths(k)[way]
                    if step >= length:
                        continue
                    if way == 0:
                        dest = (here + length - step) % RING
                    else:
                        dest = (here + RING - length + step) % RING
                    term = partial[h, dest, k]
                    if step == 0:
                        ring_out[h, way, k] = term.astype(BF16)
                    else:
                        ring_copy(h, way, step - 1, k).wait_recv()
                        ring_in[h, way, step - 1, k] = (
                            ring_in[h, way, step - 1, k].astype(F32) + term
                        ).astype(BF16)
                    ring_copy(h, way, step, k).start()
        if step == 0:
            target_rows = rows[:, :, basis:].reshape(depth, 128)
            for c in range(RING):
                rhs_part[c] = lax.dot_general(
                    target_rows, right_block(c), contract, preferred_element_type=F32
                )[:8]
            for to in range(1, RING):
                rhs_copy_z(to).start()
            for q in range(CHUNKS):
                for side in range(2):
                    ghost_copy(side, q).wait_send()
                for kind in range(9):
                    x_copy(kind, q).wait_send()
        if step == 1:
            total = rhs_part[z]
            for back in range(1, RING):
                rhs_copy_z(back).wait_recv()
                total = total + rhs_in_z[back - 1]
            rhs_mid[...] = total
            for to in range(1, RING):
                rhs_copy_y(to).start()

    def second_copy(h, k):
        if h == 0:
            to_z = (y + OFFSETS[k]) % RING
            offset = (to_z + RING - z) % RING
            to = device(x, y, to_z, core)
        else:
            to_y = (z + RING - OFFSETS[k]) % RING
            offset = (to_y + RING - y) % RING
            to = device(x, to_y, z, core)
        return remote(
            second_out.at[h, k],
            second_in.at[h, offset],
            second_send.at[h, k],
            second_recv.at[h, offset],
            to,
        )

    for k in range(BLOCKS):
        for h in range(2):
            here = y if h == 0 else z
            total = partial[h, here, k]
            for way in range(2):
                length = chain_lengths(k)[way]
                ring_copy(h, way, length - 1, k).wait_recv()
                total = total + ring_in[h, way, length - 1, k].astype(F32)

            @pl.when(delta == OFFSETS[k])
            def _():
                kept[h] = total

            @pl.when(delta != OFFSETS[k])
            def _():
                second_out[h, k] = total.astype(BF16)
                second_copy(h, k).start()

    total = rhs_mid[...]
    for step in range(1, RING):
        rhs_copy_y(step).wait_recv()
        total = total + rhs_in_y[step - 1]
    rhs_ref[...] = total[:1]

    def mirror_copy(h):
        return remote(
            mirror_out.at[h],
            mirror_in.at[core],
            mirror_send.at[h],
            mirror_recv.at[core],
            device(mirror_x, z, y, h),
        )

    def second_arrival(h, offset):
        return remote(
            second_out.at[h, 0],
            second_in.at[h, offset],
            second_send.at[h, 0],
            second_recv.at[h, offset],
            sibling,
        )

    for k in range(BLOCKS):
        for h in range(2):
            for way in range(2):
                for step in range(chain_lengths(k)[way]):
                    ring_copy(h, way, step, k).wait_send()
    for step in range(1, RING):
        rhs_copy_z(step).wait_send()
        rhs_copy_y(step).wait_send()

    @pl.when(jnp.logical_not(takes_mirror))
    def _():
        for h in range(2):
            total = kept[h]
            for offset in range(1, RING):
                second_arrival(h, offset).wait_recv()
                total = total + second_in[h, offset].astype(F32)
            gram_ref[h * 128 : (h + 1) * 128, :] = total
            mirror_out[h] = total.T

            @pl.when(sends_mirror)
            def _():
                mirror_copy(h).start()

    @pl.when(takes_mirror)
    def _():
        for sender in range(2):
            remote(
                mirror_out.at[0],
                mirror_in.at[sender],
                mirror_send.at[0],
                mirror_recv.at[sender],
                sibling,
            ).wait_recv()
            gram_ref[sender * 128 : (sender + 1) * 128, :] = mirror_in[sender]

    for k in range(BLOCKS):
        for h in range(2):

            @pl.when(delta != OFFSETS[k])
            def _():
                second_copy(h, k).wait_send()

    @pl.when(sends_mirror)
    def _():
        for h in range(2):
            mirror_copy(h).wait_send()


def per_device(pair_blocks, pair_target, ghost_source, weight_code, ref_forces):
    _, pair_count, comps, basis = pair_blocks.shape
    atoms = weight_code.shape[1]
    width = basis // CHUNKS
    dom_count = lax.axis_size("dom")
    grp_count = lax.axis_size("grp")
    factor = 1.0 / math.sqrt(comps * atoms * dom_count * grp_count)
    dma = pltpu.SemaphoreType.DMA
    vmem = pl.BlockSpec(memory_space=pltpu.VMEM)
    gram, rhs = pl.pallas_call(
        kernel,
        out_shape=(
            jax.ShapeDtypeStruct((256, 128), F32),
            jax.ShapeDtypeStruct((1, 128), F32),
        ),
        in_specs=[
            pl.BlockSpec(memory_space=pl.ANY),
        ]
        * 5,
        out_specs=(vmem, vmem),
        scratch_shapes=[
            pltpu.VMEM((1, pair_count), jnp.int32),
            pltpu.SMEM((2, atoms // 2), jnp.int32),
            pltpu.VMEM((1, atoms), jnp.int32),
            pltpu.VMEM((comps, 1, atoms), F32),
            pltpu.VMEM((comps, pair_count, basis), BF16),
            pltpu.VMEM((comps, atoms, basis), F32),
            pltpu.VMEM((CHUNKS, 2, 16, width * 3 // 2), BF16),
            pltpu.VMEM((CHUNKS, 32, width * 3 // 2), BF16),
            pltpu.VMEM((2 * XS, comps * atoms, basis + 128), BF16),
            pltpu.VMEM((2, RING, BLOCKS, 128, 128), F32),
            pltpu.VMEM((2, 2, BLOCKS, 128, 128), BF16),
            pltpu.VMEM((2, 2, 4, BLOCKS, 128, 128), BF16),
            pltpu.VMEM((2, 128, 128), F32),
            pltpu.VMEM((2, BLOCKS, 128, 128), BF16),
            pltpu.VMEM((2, RING, 128, 128), BF16),
            pltpu.VMEM((2, 128, 128), F32),
            pltpu.VMEM((2, 128, 128), F32),
            pltpu.VMEM((RING, 8, 128), F32),
            pltpu.VMEM((RING - 1, 8, 128), F32),
            pltpu.VMEM((8, 128), F32),
            pltpu.VMEM((RING - 1, 8, 128), F32),
            dma((CHUNKS,)),
            dma((4,)),
            dma((2, CHUNKS)),
            dma((2, CHUNKS)),
            dma((9, CHUNKS)),
            dma((9, CHUNKS)),
            dma((2, 2, 4, BLOCKS)),
            dma((2, 2, 4, BLOCKS)),
            dma((2, BLOCKS)),
            dma((2, RING)),
            dma((2,)),
            dma((2,)),
            dma((2, RING - 1)),
            dma((2, RING - 1)),
        ],
        compiler_params=pltpu.CompilerParams(
            collective_id=0,
            has_side_effects=True,
            vmem_limit_bytes=60 * 1024 * 1024,
        ),
    )(
        jnp.transpose(pair_blocks[0], (1, 0, 2)),
        pair_target,
        ghost_source[0, 0],
        weight_code,
        jnp.transpose(ref_forces, (2, 0, 1)),
    )
    return gram * factor, rhs.reshape(128) * factor


def solution(mesh):
    return jax.shard_map(
        per_device,
        mesh=mesh,
        in_specs=(
            P("grp", "dom", None, None),
            P("grp", "dom"),
            P("grp", "dom", None, None),
            P("grp", "dom"),
            P("grp", "dom", None),
        ),
        out_specs=(P("grp", "dom"), P("dom")),
        check_vma=False,
    )
```

```python
import functools
import math

import jax
import jax.numpy as jnp
from jax import lax
from jax.experimental import pallas as pl
from jax.experimental.pallas import tpu as pltpu
from jax.sharding import PartitionSpec as P

MESH = pl.DeviceIdType.MESH
RING = 8
XS = 4
OFFSETS = (1, 3, 6, 0, 4)
BLOCKS = len(OFFSETS)
CHUNKS = 4
F32 = jnp.float32
BF16 = jnp.bfloat16


ORDER = ((0, 2, 4), (1, 3))
CHUNKS = 4
F32 = jnp.float32
BF16 = jnp.bfloat16


GROUPS = ((0, 3, (4, 3)), (3, 2, (3, 4)))


def chain_lengths(k):
    return (4, 3) if k % 2 == 0 else (3, 4)


def kernel(
    blocks,
    target_hbm,
    ghost_hbm,
    weight_hbm,
    force_hbm,
    gram_ref,
    rhs_ref,
    target_ref,
    ghost_ref,
    weight_ref,
    force_ref,
    pairs,
    own,
    ghost_out,
    ghost_in,
    rows,
    partial,
    ring_out,
    ring_in,
    kept,
    second_out,
    second_in,
    mirror_out,
    mirror_in,
    rhs_part,
    rhs_in_z,
    rhs_mid,
    rhs_in_y,
    load_sem,
    small_sem,
    ghost_send,
    ghost_recv,
    x_send,
    x_recv,
    sib_recv,
    ring_send,
    ring_recv,
    second_send,
    second_recv,
    mirror_send,
    mirror_recv,
    rhs_send,
    rhs_recv,
):
    basis = blocks.shape[2]
    pair_count = blocks.shape[1]
    atoms = weight_ref.shape[1]
    half_basis = basis // 2
    width = basis // CHUNKS
    half_width = width // 2

    g = lax.axis_index("grp")
    d = lax.axis_index("dom")
    xl, y = g // RING, g % RING
    xh, z, core = d // (2 * RING), (d // 2) % RING, d % 2
    x = xh * 2 + xl
    delta = (z - y + RING) % RING

    def device(x_, y_, z_, core_):
        return {
            "grp": (x_ % 2) * RING + y_,
            "dom": (x_ // 2) * (2 * RING) + z_ * 2 + core_,
        }

    sibling = device(x, y, z, 1 - core)
    right = device((x + 1) % XS, y, z, core)
    left = device((x + XS - 1) % XS, y, z, core)
    dom_count = 4 * RING
    below = {"grp": g, "dom": (d + dom_count - 1) % dom_count}
    above = {"grp": g, "dom": (d + 1) % dom_count}
    off_chip = {"grp": g, "dom": (d + dom_count - 1 + 2 * core) % dom_count}
    mirror_x = (x % 2) * 2 + x // 2

    def remote(src, dst, send_sem, recv_sem, to):
        return pltpu.make_async_remote_copy(
            src_ref=src,
            dst_ref=dst,
            send_sem=send_sem,
            recv_sem=recv_sem,
            device_id=to,
            device_id_type=MESH,
        )

    def landed(ref, sem):
        remote(ref, ref, sem, sem, sibling).wait_recv()

    def gone(ref, sem):
        remote(ref, ref, sem, sem, sibling).wait_send()

    def load(q):
        columns = pl.ds(q * width, width)
        return pltpu.make_async_copy(
            blocks.at[:, :, columns], pairs.at[:, :, columns], load_sem.at[q]
        )

    small_loads = [
        pltpu.make_async_copy(source, place, small_sem.at[i])
        for i, (source, place) in enumerate(
            (
                (target_hbm, target_ref),
                (ghost_hbm, ghost_ref),
                (weight_hbm, weight_ref),
                (force_hbm, force_ref),
            )
        )
    ]
    for copy in small_loads:
        copy.start()
    for q in range(CHUNKS):
        load(q).start()

    barrier = pltpu.get_barrier_semaphore()

    def greet(to):
        pl.semaphore_signal(barrier, inc=1, device_id=to, device_id_type=MESH)

    up, down = (device(x, (y + by) % RING, z, core) for by in (1, RING - 1))
    greeted = (off_chip, sibling, right, left, up, down)
    for to in greeted:
        greet(to)

    sends_mirror = (delta == OFFSETS[0]) | (delta == OFFSETS[1]) | (delta == OFFSETS[2])
    takes_mirror = jnp.logical_not(sends_mirror) & (delta % 4 != 0)

    for copy in small_loads:
        copy.wait()

    slots = 2 * atoms
    per_atom = pair_count // atoms
    slot_ids = lax.broadcasted_iota(jnp.int32, (slots, pair_count), 0)
    pair_ids = lax.broadcasted_iota(jnp.int32, (slots, pair_count), 1)
    center = pair_ids // per_atom
    signs = (
        (slot_ids == center).astype(F32) - (slot_ids == target_ref[...]).astype(F32)
    ).astype(BF16)

    ghosts = atoms // 2
    row_ids = lax.broadcasted_iota(jnp.int32, (2 * atoms, 2 * atoms), 0)
    col_ids = lax.broadcasted_iota(jnp.int32, (2 * atoms, 2 * atoms), 1)
    source = jnp.zeros((2 * atoms, 2 * atoms), jnp.int32)
    for side in range(2):
        for ghost in range(ghosts):
            here = (col_ids // atoms == side) & (col_ids % ghosts == ghost)
            source = jnp.where(here, ghost_ref[side, ghost], source)
    placed = (row_ids % atoms == source) & (
        row_ids // atoms == (col_ids // ghosts) % 2
    )
    placed = placed.astype(F32).astype(BF16)

    diagonal = lax.broadcasted_iota(jnp.int32, (atoms, atoms), 0) == (
        lax.broadcasted_iota(jnp.int32, (atoms, atoms), 1)
    )

    def as_column(row):
        return jnp.sum(jnp.where(diagonal, row, 0.0), axis=1, keepdims=True)

    scale = as_column((1.0 + weight_ref[...].astype(F32)) * 0.5)
    first_lane = lax.broadcasted_iota(jnp.int32, (atoms, 128), 1) == 0
    my_slot = x * 2 + core
    for comp in range(3):
        column = as_column(force_ref[comp]) * scale
        rows[my_slot, comp * atoms : (comp + 1) * atoms, basis:] = jnp.where(
            first_lane, column, 0.0
        ).astype(BF16)

    def ghost_copy(side, q):
        return remote(
            ghost_out.at[q, side],
            ghost_in.at[q, pl.ds(side * 16, 16)],
            ghost_send.at[0],
            ghost_recv.at[q],
            below if side == 0 else above,
        )

    def slots_of(q):
        load(q).wait()
        columns = pl.ds(q * width, width)
        ghost_rows = []
        for comp in range(3):
            slot_rows = jnp.dot(signs, pairs[comp, :, columns], preferred_element_type=F32)
            own[comp, :, columns] = slot_rows[:atoms]
            ghost_rows.append(slot_rows[atoms:])
        for side in range(2):
            part = [rows_[side * ghosts : (side + 1) * ghosts] for rows_ in ghost_rows]
            ghost_out[q, side, :, :width] = jnp.concatenate(part[:2], axis=0).astype(BF16)
            ghost_out[q, side, :, width:] = jnp.concatenate(
                [part[2][:, :half_width], part[2][:, half_width:]], axis=0
            ).astype(BF16)
        if q == 0:
            pl.semaphore_wait(barrier, len(greeted))
        for side in range(2):
            ghost_copy(side, q).start()

    def span(q, part):
        start, stop = q * width, (q + 1) * width
        middle = start + half_width
        if q == CHUNKS - 1:
            stop = stop + 128
        if part == 0:
            stop = middle
        elif part == 1:
            start = middle
        return pl.ds(start, stop - start)

    slot_right = ((x + 1) % XS) * 2
    slot_left = ((x + XS - 1) % XS) * 2
    slot_far = ((x + 2) % XS) * 2

    def x_copy(kind, q):
        slot, part, to = (
            (my_slot, None, sibling),
            (my_slot, None, right),
            (my_slot, None, left),
            (slot_left + core, None, sibling),
            (slot_right + core, None, sibling),
            (slot_left + core, 0, right),
            (slot_right + core, 1, left),
            (slot_far + core, 0, sibling),
            (slot_far + core, 1, sibling),
        )[kind]
        piece = rows.at[slot, :, span(q, part)]
        if kind in (1, 2, 5, 6):
            recv = x_recv.at[(1, 2, 5, 6).index(kind), q]
        else:
            recv = sib_recv.at[0]
        return remote(piece, piece, x_send.at[0], recv, to)

    def design_of(q):
        columns = pl.ds(q * width, width)
        landed(ghost_in.at[q], ghost_recv.at[q])
        placed_rows = jnp.dot(placed, ghost_in[q], preferred_element_type=F32)
        for comp in range(3):
            if comp < 2:
                added = placed_rows[comp * atoms : (comp + 1) * atoms, :width]
            else:
                added = jnp.concatenate(
                    [placed_rows[:atoms, width:], placed_rows[atoms:, width:]], axis=1
                )
            rows[my_slot, comp * atoms : (comp + 1) * atoms, columns] = (
                (own[comp, :, columns] + added) * scale
            ).astype(BF16)
        for kind in (1, 2, 0):
            x_copy(kind, q).start()

    for q in range(CHUNKS):
        slots_of(q)
    for q in range(CHUNKS):
        design_of(q)

    for q in range(CHUNKS):
        for kind, relays in ((1, (5, 3)), (2, (6, 4))):
            x_copy(kind, q).wait_recv()
            for relay in relays:
                x_copy(relay, q).start()
    for q in range(CHUNKS):
        for kind, relay in ((5, 7), (6, 8)):
            x_copy(kind, q).wait_recv()
            x_copy(relay, q).start()
    landed(rows.at[pl.ds(0, 4)], sib_recv.at[0])

    contract = (((0,), (0,)), ((), ()))
    depth = rows.shape[0] * rows.shape[1]

    def right_block(c):
        start = pl.multiple_of(xh * half_basis + (2 * c + core) * 128, 128)
        return rows[:, :, pl.ds(start, 128)].reshape(depth, 128)

    def left_block(h, r):
        start = pl.multiple_of(xl * half_basis + (2 * r + h) * 128, 128)
        return rows[:, :, pl.ds(start, 128)].reshape(depth, 128)

    def product(by):
        r = (y + by + RING) % RING
        right_blocks = jnp.concatenate(
            [right_block((r + offset) % RING) for offset in OFFSETS], axis=1
        )
        tile = lax.dot_general(
            left_block(0, r), right_blocks, contract, preferred_element_type=F32
        )
        for k in range(BLOCKS):
            partial[0, r, k] = tile[:, k * 128 : (k + 1) * 128]
        c = (z + by + RING) % RING
        left_blocks = jnp.concatenate(
            [left_block(1, (c + RING - offset) % RING) for offset in OFFSETS], axis=1
        )
        tile = lax.dot_general(
            right_block(c), left_blocks, contract, preferred_element_type=F32
        )
        for k in range(BLOCKS):
            partial[1, c, k] = tile[:, k * 128 : (k + 1) * 128]

    def rhs_copy_z(step):
        to_z = (z + step) % RING
        return remote(
            rhs_part.at[to_z],
            rhs_in_z.at[step - 1],
            rhs_send.at[0],
            rhs_recv.at[0],
            device(x, y, to_z, core),
        )

    def rhs_copy_y(step):
        return remote(
            rhs_mid,
            rhs_in_y.at[step - 1],
            rhs_send.at[1],
            rhs_recv.at[1],
            device(x, (y + step) % RING, z, core),
        )

    ring_to = (
        (device(x, (y + 1) % RING, z, core), device(x, (y + RING - 1) % RING, z, core)),
        (device(x, y, (z + 1) % RING, core), device(x, y, (z + RING - 1) % RING, core)),
    )

    def ring_copy(h, way, step, k):
        src = ring_out.at[h, way, k] if step == 0 else ring_in.at[h, way, step - 1, k]
        return remote(
            src,
            ring_in.at[h, way, step, k],
            ring_send.at[step],
            ring_recv.at[way, step, k],
            ring_to[h][way],
        )

    def rhs_products(blocks_):
        target_rows = rows[:, :, basis:].reshape(depth, 128)[:, :16]
        for c in blocks_:
            rhs_part[c] = lax.dot_general(
                target_rows, right_block(c), contract, preferred_element_type=F32
            )[:8]

    def ring_step(step, group):
        for k in ORDER[group]:
            for way in range(2):
                length = chain_lengths(k)[way]
                if step >= length:
                    continue
                if step > 0:
                    landed(ring_in.at[:, way, step - 1, k], ring_recv.at[way, step - 1, k])
                for h in range(2):
                    here = y if h == 0 else z
                    if way == 0:
                        dest = (here + length - step) % RING
                    else:
                        dest = (here + RING - length + step) % RING
                    term = partial[h, dest, k]
                    if step == 0:
                        ring_out[h, way, k] = term.astype(BF16)
                    else:
                        ring_in[h, way, step - 1, k] = (
                            ring_in[h, way, step - 1, k].astype(F32) + term
                        ).astype(BF16)
                    ring_copy(h, way, step, k).start()

    product(4)
    product(-3)
    ring_step(0, 0)
    product(3)
    ring_step(0, 1)
    product(-2)
    ring_step(1, 0)
    product(2)
    ring_step(1, 1)
    product(-1)
    ring_step(2, 0)
    product(1)
    ring_step(2, 1)
    rhs_products(range(0, RING))
    product(0)
    ring_step(3, 0)
    gone(ghost_out, ghost_send.at[0])
    gone(rows.at[pl.ds(0, 7)], x_send.at[0])
    ring_step(3, 1)
    def second_copy(h, k):
        if h == 0:
            to_z = (y + OFFSETS[k]) % RING
            offset = (to_z + RING - z) % RING
            to = device(x, y, to_z, core)
        else:
            to_y = (z + RING - OFFSETS[k]) % RING
            offset = (to_y + RING - y) % RING
            to = device(x, to_y, z, core)
        return remote(
            second_out.at[h, k],
            second_in.at[h, offset],
            second_send.at[0],
            second_recv.at[h],
            to,
        )

    for k in ORDER[0] + ORDER[1]:
        lengths = chain_lengths(k)
        for way in range(2):
            last = lengths[way] - 1
            landed(ring_in.at[:, way, last, k], ring_recv.at[way, last, k])
        for h in range(2):
            here = y if h == 0 else z
            total = partial[h, here, k]
            for way in range(2):
                total = total + ring_in[h, way, lengths[way] - 1, k].astype(F32)

            @pl.when(delta == OFFSETS[k])
            def _():
                kept[h] = total

            @pl.when(delta != OFFSETS[k])
            def _():
                second_out[h, k] = total.astype(BF16)
                second_copy(h, k).start()

    for to in range(1, RING):
        rhs_copy_z(to).start()

    for step in range(3):
        gone(ring_in.at[:, :, step], ring_send.at[step])
    gone(ring_out.at[0], ring_send.at[3])

    def mirror_copy(h):
        return remote(
            mirror_out.at[h],
            mirror_in.at[core],
            mirror_send.at[0],
            mirror_recv.at[0],
            device(mirror_x, z, y, h),
        )

    @pl.when(jnp.logical_not(takes_mirror))
    def _():
        for h in range(2):
            total = kept[h]
            landed(second_in.at[h, pl.ds(1, RING - 1)], second_recv.at[h])
            for offset in range(1, RING):
                total = total + second_in[h, offset].astype(F32)
            flipped = total.T
            mirror_out[h] = (flipped if h == 0 else total).astype(BF16)

            @pl.when(sends_mirror)
            def _():
                mirror_copy(h).start()

            gram_ref[h * 128 : (h + 1) * 128, :] = total if h == 0 else flipped

    landed(rhs_in_z, rhs_recv.at[0])
    total = rhs_part[z]
    for back in range(1, RING):
        total = total + rhs_in_z[back - 1]
    rhs_mid[...] = total
    for to in range(1, RING):
        rhs_copy_y(to).start()

    gone(rhs_in_z, rhs_send.at[0])

    @pl.when(jnp.logical_not(takes_mirror))
    def _():
        gone(second_out.at[:, pl.ds(0, BLOCKS - 1)], second_send.at[0])

    @pl.when(takes_mirror)
    def _():
        gone(second_out, second_send.at[0])
        landed(mirror_in, mirror_recv.at[0])
        for sender in range(2):
            gram_ref[sender * 128 : (sender + 1) * 128, :] = mirror_in[sender].astype(F32)

    landed(rhs_in_y, rhs_recv.at[1])
    total = rhs_mid[...]
    for back in range(1, RING):
        total = total + rhs_in_y[back - 1]
    rhs_ref[...] = total[:1]
    gone(rhs_in_y, rhs_send.at[1])

    @pl.when(sends_mirror)
    def _():
        gone(mirror_out, mirror_send.at[0])


def per_device(pair_blocks, pair_target, ghost_source, weight_code, ref_forces):
    _, pair_count, comps, basis = pair_blocks.shape
    atoms = weight_code.shape[1]
    width = basis // CHUNKS
    dom_count = lax.axis_size("dom")
    grp_count = lax.axis_size("grp")
    factor = 1.0 / math.sqrt(comps * atoms * dom_count * grp_count)
    dma = pltpu.SemaphoreType.DMA
    vmem = pl.BlockSpec(memory_space=pltpu.VMEM)
    gram, rhs = pl.pallas_call(
        kernel,
        out_shape=(
            jax.ShapeDtypeStruct((256, 128), F32),
            jax.ShapeDtypeStruct((1, 128), F32),
        ),
        in_specs=[
            pl.BlockSpec(memory_space=pl.ANY),
        ]
        * 5,
        out_specs=(vmem, vmem),
        scratch_shapes=[
            pltpu.VMEM((1, pair_count), jnp.int32),
            pltpu.SMEM((2, atoms // 2), jnp.int32),
            pltpu.VMEM((1, atoms), jnp.int32),
            pltpu.VMEM((comps, 1, atoms), F32),
            pltpu.VMEM((comps, pair_count, basis), BF16),
            pltpu.VMEM((comps, atoms, basis), F32),
            pltpu.VMEM((CHUNKS, 2, 16, width * 3 // 2), BF16),
            pltpu.VMEM((CHUNKS, 32, width * 3 // 2), BF16),
            pltpu.VMEM((2 * XS, comps * atoms, basis + 128), BF16),
            pltpu.VMEM((2, RING, BLOCKS, 128, 128), F32),
            pltpu.VMEM((2, 2, BLOCKS, 128, 128), BF16),
            pltpu.VMEM((2, 2, 4, BLOCKS, 128, 128), BF16),
            pltpu.VMEM((2, 128, 128), F32),
            pltpu.VMEM((2, BLOCKS, 128, 128), BF16),
            pltpu.VMEM((2, RING, 128, 128), BF16),
            pltpu.VMEM((2, 128, 128), BF16),
            pltpu.VMEM((2, 128, 128), BF16),
            pltpu.VMEM((RING, 8, 128), F32),
            pltpu.VMEM((RING - 1, 8, 128), F32),
            pltpu.VMEM((8, 128), F32),
            pltpu.VMEM((RING - 1, 8, 128), F32),
            dma((CHUNKS,)),
            dma((4,)),
            dma((1,)),
            dma((CHUNKS,)),
            dma((1,)),
            dma((4, CHUNKS)),
            dma((1,)),
            dma((4,)),
            dma((2, 4, BLOCKS)),
            dma((1,)),
            dma((2,)),
            dma((1,)),
            dma((1,)),
            dma((2,)),
            dma((2,)),
        ],
        compiler_params=pltpu.CompilerParams(
            collective_id=0,
            has_side_effects=True,
            vmem_limit_bytes=60 * 1024 * 1024,
        ),
    )(
        jnp.transpose(pair_blocks[0], (1, 0, 2)),
        pair_target,
        ghost_source[0, 0],
        weight_code,
        jnp.transpose(ref_forces, (2, 0, 1)),
    )
    return gram * factor, rhs.reshape(128) * factor


def solution(mesh):
    return jax.shard_map(
        per_device,
        mesh=mesh,
        in_specs=(
            P("grp", "dom", None, None),
            P("grp", "dom"),
            P("grp", "dom", None, None),
            P("grp", "dom"),
            P("grp", "dom", None),
        ),
        out_specs=(P("grp", "dom"), P("dom")),
        check_vma=False,
    )
```

```python
import functools
import math

import jax
import jax.numpy as jnp
from jax import lax
from jax.experimental import pallas as pl
from jax.experimental.pallas import tpu as pltpu
from jax.sharding import PartitionSpec as P

MESH = pl.DeviceIdType.MESH
RING = 8
XS = 4
OFFSETS = (6, 0, 3, 4, 1)
MIRRORED = (1, 3, 6)
BLOCKS = len(OFFSETS)
ORDER = ((0, 2, 4), (1, 3))
RHS_HOPS = (4, 3)
CHUNKS = 4
F32 = jnp.float32
BF16 = jnp.bfloat16


def chain_lengths(k):
    return (4, 3) if k % 2 == 0 else (3, 4)


def kernel(
    blocks,
    target_hbm,
    ghost_hbm,
    weight_hbm,
    force_hbm,
    gram_ref,
    target_ref,
    ghost_ref,
    weight_ref,
    force_ref,
    pairs,
    own,
    ghost_out,
    ghost_in,
    rows,
    partial,
    ring_out,
    ring_in,
    kept,
    second_out,
    second_in,
    mirror_out,
    mirror_in,
    rhs_ring_out,
    rhs_ring_in,
    rhs_mid,
    rhs_in_y,
    load_sem,
    small_sem,
    ghost_send,
    ghost_recv,
    x_send,
    x_recv,
    sib_recv,
    ring_send,
    ring_recv,
    second_send,
    second_recv,
    mirror_send,
    mirror_recv,
    rhs_send,
    rhs_ring_recv,
    rhs_recv,
):
    basis = blocks.shape[2]
    pair_count = blocks.shape[1]
    atoms = weight_ref.shape[1]
    half_basis = basis // 2
    width = basis // CHUNKS
    half_width = width // 2

    g = lax.axis_index("grp")
    d = lax.axis_index("dom")
    xl, y = g // RING, g % RING
    xh, z, core = d // (2 * RING), (d // 2) % RING, d % 2
    x = xh * 2 + xl
    delta = (z - y + RING) % RING

    def device(x_, y_, z_, core_):
        return {
            "grp": (x_ % 2) * RING + y_,
            "dom": (x_ // 2) * (2 * RING) + z_ * 2 + core_,
        }

    sibling = device(x, y, z, 1 - core)
    right = device((x + 1) % XS, y, z, core)
    left = device((x + XS - 1) % XS, y, z, core)
    dom_count = 4 * RING
    below = {"grp": g, "dom": (d + dom_count - 1) % dom_count}
    above = {"grp": g, "dom": (d + 1) % dom_count}
    off_chip = {"grp": g, "dom": (d + dom_count - 1 + 2 * core) % dom_count}
    mirror_x = (x % 2) * 2 + x // 2

    def remote(src, dst, send_sem, recv_sem, to):
        return pltpu.make_async_remote_copy(
            src_ref=src,
            dst_ref=dst,
            send_sem=send_sem,
            recv_sem=recv_sem,
            device_id=to,
            device_id_type=MESH,
        )

    def landed(ref, sem):
        remote(ref, ref, sem, sem, sibling).wait_recv()

    def gone(ref, sem):
        remote(ref, ref, sem, sem, sibling).wait_send()

    def load(q):
        columns = pl.ds(q * width, width)
        return pltpu.make_async_copy(
            blocks.at[:, :, columns], pairs.at[:, :, columns], load_sem.at[q]
        )

    small_loads = [
        pltpu.make_async_copy(source, place, small_sem.at[i])
        for i, (source, place) in enumerate(
            (
                (target_hbm, target_ref),
                (ghost_hbm, ghost_ref),
                (weight_hbm, weight_ref),
                (force_hbm, force_ref),
            )
        )
    ]
    for copy in small_loads:
        copy.start()
    for q in range(CHUNKS):
        load(q).start()

    barrier = pltpu.get_barrier_semaphore()

    def greet(to):
        pl.semaphore_signal(barrier, inc=1, device_id=to, device_id_type=MESH)

    up, down = (device(x, (y + by) % RING, z, core) for by in (1, RING - 1))
    greeted = (off_chip, sibling, right, left, up, down)
    for to in greeted:
        greet(to)

    sends_mirror = (delta == MIRRORED[0]) | (delta == MIRRORED[1]) | (delta == MIRRORED[2])
    takes_mirror = jnp.logical_not(sends_mirror) & (delta % 4 != 0)

    for copy in small_loads:
        copy.wait()

    slots = 2 * atoms
    per_atom = pair_count // atoms
    slot_ids = lax.broadcasted_iota(jnp.int32, (slots, pair_count), 0)
    pair_ids = lax.broadcasted_iota(jnp.int32, (slots, pair_count), 1)
    center = pair_ids // per_atom
    signs = (
        (slot_ids == center).astype(F32) - (slot_ids == target_ref[...]).astype(F32)
    ).astype(BF16)

    ghosts = atoms // 2
    row_ids = lax.broadcasted_iota(jnp.int32, (2 * atoms, 2 * atoms), 0)
    col_ids = lax.broadcasted_iota(jnp.int32, (2 * atoms, 2 * atoms), 1)
    source = jnp.zeros((2 * atoms, 2 * atoms), jnp.int32)
    for side in range(2):
        for ghost in range(ghosts):
            here = (col_ids // atoms == side) & (col_ids % ghosts == ghost)
            source = jnp.where(here, ghost_ref[side, ghost], source)
    placed = (row_ids % atoms == source) & (
        row_ids // atoms == (col_ids // ghosts) % 2
    )
    placed = placed.astype(F32).astype(BF16)

    diagonal = lax.broadcasted_iota(jnp.int32, (atoms, atoms), 0) == (
        lax.broadcasted_iota(jnp.int32, (atoms, atoms), 1)
    )

    def as_column(row):
        return jnp.sum(jnp.where(diagonal, row, 0.0), axis=1, keepdims=True)

    scale = as_column((1.0 + weight_ref[...].astype(F32)) * 0.5)
    first_lane = lax.broadcasted_iota(jnp.int32, (atoms, 128), 1) == 0
    my_slot = x * 2 + core
    for comp in range(3):
        column = as_column(force_ref[comp]) * scale
        rows[my_slot, comp * atoms : (comp + 1) * atoms, basis:] = jnp.where(
            first_lane, column, 0.0
        ).astype(BF16)

    def ghost_copy(side, q):
        return remote(
            ghost_out.at[q, side],
            ghost_in.at[q, pl.ds(side * 16, 16)],
            ghost_send.at[0],
            ghost_recv.at[q],
            below if side == 0 else above,
        )

    def slots_of(q):
        load(q).wait()
        columns = pl.ds(q * width, width)
        ghost_rows = []
        for comp in range(3):
            slot_rows = jnp.dot(signs, pairs[comp, :, columns], preferred_element_type=F32)
            own[comp, :, columns] = slot_rows[:atoms]
            ghost_rows.append(slot_rows[atoms:])
        for side in range(2):
            part = [rows_[side * ghosts : (side + 1) * ghosts] for rows_ in ghost_rows]
            ghost_out[q, side, :, :width] = jnp.concatenate(part[:2], axis=0).astype(BF16)
            ghost_out[q, side, :, width:] = jnp.concatenate(
                [part[2][:, :half_width], part[2][:, half_width:]], axis=0
            ).astype(BF16)
        if q == 0:
            pl.semaphore_wait(barrier, len(greeted))
        for side in range(2):
            ghost_copy(side, q).start()

    def span(q, part):
        start, stop = q * width, (q + 1) * width
        middle = start + half_width
        if q == CHUNKS - 1:
            stop = stop + 128
        if part == 0:
            stop = middle
        elif part == 1:
            start = middle
        return pl.ds(start, stop - start)

    slot_right = ((x + 1) % XS) * 2
    slot_left = ((x + XS - 1) % XS) * 2
    slot_far = ((x + 2) % XS) * 2

    def x_copy(kind, q):
        slot, part, to = (
            (my_slot, None, sibling),
            (my_slot, None, right),
            (my_slot, None, left),
            (slot_left + core, None, sibling),
            (slot_right + core, None, sibling),
            (slot_left + core, 0, right),
            (slot_right + core, 1, left),
            (slot_far + core, 0, sibling),
            (slot_far + core, 1, sibling),
        )[kind]
        piece = rows.at[slot, :, span(q, part)]
        if kind in (1, 2, 5, 6):
            recv = x_recv.at[(1, 2, 5, 6).index(kind), q]
        else:
            recv = sib_recv.at[0]
        return remote(piece, piece, x_send.at[0], recv, to)

    def design_of(q):
        columns = pl.ds(q * width, width)
        landed(ghost_in.at[q], ghost_recv.at[q])
        placed_rows = jnp.dot(placed, ghost_in[q], preferred_element_type=F32)
        for comp in range(3):
            if comp < 2:
                added = placed_rows[comp * atoms : (comp + 1) * atoms, :width]
            else:
                added = jnp.concatenate(
                    [placed_rows[:atoms, width:], placed_rows[atoms:, width:]], axis=1
                )
            rows[my_slot, comp * atoms : (comp + 1) * atoms, columns] = (
                (own[comp, :, columns] + added) * scale
            ).astype(BF16)
        for kind in (1, 2, 0):
            x_copy(kind, q).start()

    for q in range(CHUNKS):
        slots_of(q)
    for q in range(CHUNKS):
        design_of(q)

    for q in range(CHUNKS):
        for kind, relays in ((1, (5, 3)), (2, (6, 4))):
            x_copy(kind, q).wait_recv()
            for relay in relays:
                x_copy(relay, q).start()
    for q in range(CHUNKS):
        for kind, relay in ((5, 7), (6, 8)):
            x_copy(kind, q).wait_recv()
            x_copy(relay, q).start()
    landed(rows.at[pl.ds(0, 4)], sib_recv.at[0])

    contract = (((0,), (0,)), ((), ()))
    depth = rows.shape[0] * rows.shape[1]

    def right_block(c):
        start = pl.multiple_of(xh * half_basis + (2 * c + core) * 128, 128)
        return rows[:, :, pl.ds(start, 128)].reshape(depth, 128)

    def left_block(h, r):
        start = pl.multiple_of(xl * half_basis + (2 * r + h) * 128, 128)
        return rows[:, :, pl.ds(start, 128)].reshape(depth, 128)

    def product(by):
        r = (y + by + RING) % RING
        right_blocks = jnp.concatenate(
            [right_block((r + offset) % RING) for offset in OFFSETS], axis=1
        )
        tile = lax.dot_general(
            left_block(0, r), right_blocks, contract, preferred_element_type=F32
        )
        for k in range(BLOCKS):
            partial[0, r, k] = tile[:, k * 128 : (k + 1) * 128]
        c = (z + by + RING) % RING
        left_blocks = jnp.concatenate(
            [left_block(1, (c + RING - offset) % RING) for offset in OFFSETS], axis=1
        )
        tile = lax.dot_general(
            right_block(c), left_blocks, contract, preferred_element_type=F32
        )
        for k in range(BLOCKS):
            partial[1, c, k] = tile[:, k * 128 : (k + 1) * 128]

    ring_to = (
        (device(x, (y + 1) % RING, z, core), device(x, (y + RING - 1) % RING, z, core)),
        (device(x, y, (z + 1) % RING, core), device(x, y, (z + RING - 1) % RING, core)),
    )

    def rhs_copy_z(way, step):
        return remote(
            rhs_ring_out.at[way] if step == 0 else rhs_ring_in.at[way, step - 1],
            rhs_ring_in.at[way, step],
            rhs_send.at[0],
            rhs_ring_recv.at[way, step],
            ring_to[1][way],
        )

    def rhs_copy_y(step):
        return remote(
            rhs_mid,
            rhs_in_y.at[step - 1],
            rhs_send.at[1],
            rhs_recv.at[0],
            device(x, (y + step) % RING, z, core),
        )

    def ring_copy(h, way, step, k):
        src = ring_out.at[h, way, k] if step == 0 else ring_in.at[h, way, step - 1, k]
        return remote(
            src,
            ring_in.at[h, way, step, k],
            ring_send.at[step],
            ring_recv.at[way, step, k],
            ring_to[h][way],
        )

    def rhs_term(by):
        target_rows = rows[:, :, basis:].reshape(depth, 128)[:, :16]
        c = (z + by + RING) % RING
        return lax.dot_general(
            target_rows, right_block(c), contract, preferred_element_type=F32
        )[:8]

    def rhs_step(step):
        for way, length in enumerate(RHS_HOPS):
            if step >= length:
                continue
            term = rhs_term(length - step if way == 0 else step - length)
            if step == 0:
                rhs_ring_out[way] = term
            else:
                landed(rhs_ring_in.at[way, step - 1], rhs_ring_recv.at[way, step - 1])
                rhs_ring_in[way, step - 1] = rhs_ring_in[way, step - 1] + term
            rhs_copy_z(way, step).start()

    def ring_step(step, group):
        for k in ORDER[group]:
            for way in range(2):
                length = chain_lengths(k)[way]
                if step >= length:
                    continue
                if step > 0:
                    landed(ring_in.at[:, way, step - 1, k], ring_recv.at[way, step - 1, k])
                for h in range(2):
                    here = y if h == 0 else z
                    if way == 0:
                        dest = (here + length - step) % RING
                    else:
                        dest = (here + RING - length + step) % RING
                    term = partial[h, dest, k]
                    if step == 0:
                        ring_out[h, way, k] = term.astype(BF16)
                    else:
                        ring_in[h, way, step - 1, k] = (
                            ring_in[h, way, step - 1, k].astype(F32) + term
                        ).astype(BF16)
                    ring_copy(h, way, step, k).start()

    product(4)
    product(-3)
    ring_step(0, 0)
    product(3)
    ring_step(0, 1)
    product(-2)
    ring_step(1, 0)
    product(2)
    ring_step(1, 1)
    rhs_step(0)
    product(-1)
    ring_step(2, 0)
    product(1)
    rhs_step(1)
    ring_step(2, 1)
    product(0)
    gone(ghost_out, ghost_send.at[0])
    gone(rows.at[pl.ds(0, 7)], x_send.at[0])
    rhs_step(2)
    ring_step(3, 0)
    rhs_mid[...] = rhs_term(0)
    rhs_step(3)
    ring_step(3, 1)

    def second_copy(h, k):
        if h == 0:
            to_z = (y + OFFSETS[k]) % RING
            offset = (to_z + RING - z) % RING
            to = device(x, y, to_z, core)
        else:
            to_y = (z + RING - OFFSETS[k]) % RING
            offset = (to_y + RING - y) % RING
            to = device(x, to_y, z, core)
        return remote(
            second_out.at[h, k],
            second_in.at[h, offset],
            second_send.at[k % 2],
            second_recv.at[h],
            to,
        )

    def finish(group):
        for k in ORDER[group]:
            lengths = chain_lengths(k)
            for way in range(2):
                last = lengths[way] - 1
                landed(ring_in.at[:, way, last, k], ring_recv.at[way, last, k])
            for h in range(2):
                here = y if h == 0 else z
                total = partial[h, here, k]
                for way in range(2):
                    total = total + ring_in[h, way, lengths[way] - 1, k].astype(F32)

                @pl.when(delta == OFFSETS[k])
                def _():
                    kept[h] = total

                @pl.when(delta != OFFSETS[k])
                def _():
                    second_out[h, k] = total.astype(BF16)
                    second_copy(h, k).start()


    finish(0)
    for way, length in enumerate(RHS_HOPS):
        landed(rhs_ring_in.at[way, length - 1], rhs_ring_recv.at[way, length - 1])
        rhs_mid[...] += rhs_ring_in[way, length - 1]
    for to in range(1, RING):
        rhs_copy_y(to).start()

    @pl.when(sends_mirror)
    def _():
        gone(second_out.at[:, pl.ds(0, 2)], second_send.at[0])

    @pl.when(jnp.logical_not(sends_mirror))
    def _():
        gone(second_out.at[:, pl.ds(0, 3)], second_send.at[0])

    finish(1)

    def mirror_copy(h):
        return remote(
            mirror_out.at[h],
            mirror_in.at[core],
            mirror_send.at[0],
            mirror_recv.at[0],
            device(mirror_x, z, y, h),
        )

    @pl.when(jnp.logical_not(takes_mirror))
    def _():
        for h in range(2):
            total = kept[h]
            landed(second_in.at[h, pl.ds(1, RING - 1)], second_recv.at[h])
            for offset in range(1, RING):
                total = total + second_in[h, offset].astype(F32)
            flipped = total.T
            mirror_out[h] = (flipped if h == 0 else total).astype(BF16)

            @pl.when(sends_mirror)
            def _():
                mirror_copy(h).start()

            gram_ref[h * 128 : (h + 1) * 128, :] = total if h == 0 else flipped

    for step in range(3):
        gone(ring_in.at[:, :, step], ring_send.at[step])
    gone(ring_out.at[0], ring_send.at[3])

    gone(rhs_in_y, rhs_send.at[0])

    @pl.when(delta % 4 == 0)
    def _():
        gone(second_out.at[:, pl.ds(0, 1)], second_send.at[1])

    @pl.when(delta % 4 != 0)
    def _():
        gone(second_out.at[:, pl.ds(0, 2)], second_send.at[1])

    @pl.when(takes_mirror)
    def _():
        landed(mirror_in, mirror_recv.at[0])
        for sender in range(2):
            gram_ref[sender * 128 : (sender + 1) * 128, :] = mirror_in[sender].astype(F32)

    landed(rhs_in_y, rhs_recv.at[0])
    total = rhs_mid[...]
    for back in range(1, RING):
        total = total + rhs_in_y[back - 1]
    gram_ref[256:264] = total
    gone(rhs_in_y, rhs_send.at[1])

    @pl.when(sends_mirror)
    def _():
        gone(mirror_out, mirror_send.at[0])


def per_device(pair_blocks, pair_target, ghost_source, weight_code, ref_forces):
    _, pair_count, comps, basis = pair_blocks.shape
    atoms = weight_code.shape[1]
    width = basis // CHUNKS
    dom_count = lax.axis_size("dom")
    grp_count = lax.axis_size("grp")
    factor = 1.0 / math.sqrt(comps * atoms * dom_count * grp_count)
    dma = pltpu.SemaphoreType.DMA
    vmem = pl.BlockSpec(memory_space=pltpu.VMEM)
    (both,) = pl.pallas_call(
        kernel,
        out_shape=(
            jax.ShapeDtypeStruct((264, 128), F32),
        ),
        in_specs=[
            pl.BlockSpec(memory_space=pl.ANY),
        ]
        * 5,
        out_specs=(vmem,),
        scratch_shapes=[
            pltpu.VMEM((1, pair_count), jnp.int32),
            pltpu.SMEM((2, atoms // 2), jnp.int32),
            pltpu.VMEM((1, atoms), jnp.int32),
            pltpu.VMEM((comps, 1, atoms), F32),
            pltpu.VMEM((comps, pair_count, basis), BF16),
            pltpu.VMEM((comps, atoms, basis), F32),
            pltpu.VMEM((CHUNKS, 2, 16, width * 3 // 2), BF16),
            pltpu.VMEM((CHUNKS, 32, width * 3 // 2), BF16),
            pltpu.VMEM((2 * XS, comps * atoms, basis + 128), BF16),
            pltpu.VMEM((2, RING, BLOCKS, 128, 128), F32),
            pltpu.VMEM((2, 2, BLOCKS, 128, 128), BF16),
            pltpu.VMEM((2, 2, 4, BLOCKS, 128, 128), BF16),
            pltpu.VMEM((2, 128, 128), F32),
            pltpu.VMEM((2, BLOCKS, 128, 128), BF16),
            pltpu.VMEM((2, RING, 128, 128), BF16),
            pltpu.VMEM((2, 128, 128), BF16),
            pltpu.VMEM((2, 128, 128), BF16),
            pltpu.VMEM((2, 8, 128), F32),
            pltpu.VMEM((2, 4, 8, 128), F32),
            pltpu.VMEM((8, 128), F32),
            pltpu.VMEM((RING - 1, 8, 128), F32),
            dma((CHUNKS,)),
            dma((4,)),
            dma((1,)),
            dma((CHUNKS,)),
            dma((1,)),
            dma((4, CHUNKS)),
            dma((1,)),
            dma((4,)),
            dma((2, 4, BLOCKS)),
            dma((2,)),
            dma((2,)),
            dma((1,)),
            dma((1,)),
            dma((2,)),
            dma((2, 4)),
            dma((1,)),
        ],
        compiler_params=pltpu.CompilerParams(
            collective_id=0,
            has_side_effects=True,
            vmem_limit_bytes=60 * 1024 * 1024,
        ),
    )(
        jnp.transpose(pair_blocks[0], (1, 0, 2)),
        pair_target,
        ghost_source[0, 0],
        weight_code,
        jnp.transpose(ref_forces, (2, 0, 1)),
    )
    both = both * factor
    return both[:256], both[256]


def solution(mesh):
    return jax.shard_map(
        per_device,
        mesh=mesh,
        in_specs=(
            P("grp", "dom", None, None),
            P("grp", "dom"),
            P("grp", "dom", None, None),
            P("grp", "dom"),
            P("grp", "dom", None),
        ),
        out_specs=(P("grp", "dom"), P("dom")),
        check_vma=False,
    )
```

```python
import functools
import math

import jax
import jax.numpy as jnp
from jax import lax
from jax.experimental import pallas as pl
from jax.experimental.pallas import tpu as pltpu
from jax.sharding import PartitionSpec as P

MESH = pl.DeviceIdType.MESH
RING = 8
XS = 4
OFFSETS = (6, 0, 3, 4, 1)
MIRRORED = (1, 3, 6)
BLOCKS = len(OFFSETS)
ORDER = ((0, 2, 4), (1, 3))
RHS_HOPS = (4, 3)
CHUNKS = 4
F32 = jnp.float32
BF16 = jnp.bfloat16


def chain_lengths(k):
    return (4, 3) if k % 2 == 0 else (3, 4)


def kernel(
    blocks,
    target_hbm,
    ghost_hbm,
    weight_hbm,
    force_hbm,
    gram_ref,
    target_ref,
    ghost_ref,
    weight_ref,
    force_ref,
    pairs,
    own,
    ghost_out,
    ghost_in,
    rows,
    partial,
    ring_out,
    ring_in,
    kept,
    second_out,
    second_in,
    mirror_out,
    mirror_in,
    rhs_ring_out,
    rhs_ring_in,
    rhs_mid,
    rhs_in_y,
    load_sem,
    small_sem,
    ghost_send,
    ghost_recv,
    x_send,
    x_recv,
    sib_recv,
    ring_send,
    ring_recv,
    second_send,
    second_recv,
    mirror_send,
    mirror_recv,
    rhs_send,
    rhs_ring_recv,
    rhs_recv,
):
    basis = blocks.shape[2]
    pair_count = blocks.shape[1]
    atoms = weight_ref.shape[1]
    half_basis = basis // 2
    width = basis // CHUNKS
    half_width = width // 2

    g = lax.axis_index("grp")
    d = lax.axis_index("dom")
    xl, y = g // RING, g % RING
    xh, z, core = d // (2 * RING), (d // 2) % RING, d % 2
    x = xh * 2 + xl
    delta = (z - y + RING) % RING

    def device(x_, y_, z_, core_):
        return {
            "grp": (x_ % 2) * RING + y_,
            "dom": (x_ // 2) * (2 * RING) + z_ * 2 + core_,
        }

    sibling = device(x, y, z, 1 - core)
    right = device((x + 1) % XS, y, z, core)
    left = device((x + XS - 1) % XS, y, z, core)
    dom_count = 4 * RING
    below = {"grp": g, "dom": (d + dom_count - 1) % dom_count}
    above = {"grp": g, "dom": (d + 1) % dom_count}
    off_chip = {"grp": g, "dom": (d + dom_count - 1 + 2 * core) % dom_count}
    mirror_x = (x % 2) * 2 + x // 2

    def remote(src, dst, send_sem, recv_sem, to):
        return pltpu.make_async_remote_copy(
            src_ref=src,
            dst_ref=dst,
            send_sem=send_sem,
            recv_sem=recv_sem,
            device_id=to,
            device_id_type=MESH,
        )

    def landed(ref, sem):
        remote(ref, ref, sem, sem, sibling).wait_recv()

    def gone(ref, sem):
        remote(ref, ref, sem, sem, sibling).wait_send()

    def load(q):
        columns = pl.ds(q * width, width)
        return pltpu.make_async_copy(
            blocks.at[:, :, columns], pairs.at[:, :, columns], load_sem.at[q]
        )

    small_loads = [
        pltpu.make_async_copy(source, place, small_sem.at[i])
        for i, (source, place) in enumerate(
            (
                (target_hbm, target_ref),
                (ghost_hbm, ghost_ref),
                (weight_hbm, weight_ref),
                (force_hbm, force_ref),
            )
        )
    ]
    for copy in small_loads:
        copy.start()
    for q in range(CHUNKS):
        load(q).start()

    barrier = pltpu.get_barrier_semaphore()

    def greet(to):
        pl.semaphore_signal(barrier, inc=1, device_id=to, device_id_type=MESH)

    up, down = (device(x, (y + by) % RING, z, core) for by in (1, RING - 1))
    greeted = (off_chip, sibling, right, left, up, down)
    for to in greeted:
        greet(to)

    sends_mirror = (delta == MIRRORED[0]) | (delta == MIRRORED[1]) | (delta == MIRRORED[2])
    takes_mirror = jnp.logical_not(sends_mirror) & (delta % 4 != 0)

    for copy in small_loads:
        copy.wait()

    slots = 2 * atoms
    per_atom = pair_count // atoms
    slot_ids = lax.broadcasted_iota(jnp.int32, (slots, pair_count), 0)
    pair_ids = lax.broadcasted_iota(jnp.int32, (slots, pair_count), 1)
    center = pair_ids // per_atom
    signs = (
        (slot_ids == center).astype(F32) - (slot_ids == target_ref[...]).astype(F32)
    ).astype(BF16)

    ghosts = atoms // 2
    row_ids = lax.broadcasted_iota(jnp.int32, (2 * atoms, 2 * atoms), 0)
    col_ids = lax.broadcasted_iota(jnp.int32, (2 * atoms, 2 * atoms), 1)
    source = jnp.zeros((2 * atoms, 2 * atoms), jnp.int32)
    for side in range(2):
        for ghost in range(ghosts):
            here = (col_ids // atoms == side) & (col_ids % ghosts == ghost)
            source = jnp.where(here, ghost_ref[side, ghost], source)
    placed = (row_ids % atoms == source) & (
        row_ids // atoms == (col_ids // ghosts) % 2
    )
    placed = placed.astype(F32).astype(BF16)

    diagonal = lax.broadcasted_iota(jnp.int32, (atoms, atoms), 0) == (
        lax.broadcasted_iota(jnp.int32, (atoms, atoms), 1)
    )

    def as_column(row):
        return jnp.sum(jnp.where(diagonal, row, 0.0), axis=1, keepdims=True)

    scale = as_column((1.0 + weight_ref[...].astype(F32)) * 0.5)
    first_lane = lax.broadcasted_iota(jnp.int32, (atoms, 128), 1) == 0
    my_slot = x * 2 + core
    for comp in range(3):
        column = as_column(force_ref[comp]) * scale
        rows[my_slot, comp * atoms : (comp + 1) * atoms, basis:] = jnp.where(
            first_lane, column, 0.0
        ).astype(BF16)

    def ghost_copy(side, q):
        return remote(
            ghost_out.at[q, side],
            ghost_in.at[q, pl.ds(side * 16, 16)],
            ghost_send.at[0],
            ghost_recv.at[q],
            below if side == 0 else above,
        )

    def slots_of(q):
        load(q).wait()
        columns = pl.ds(q * width, width)
        ghost_rows = []
        for comp in range(3):
            slot_rows = jnp.dot(signs, pairs[comp, :, columns], preferred_element_type=F32)
            own[comp, :, columns] = slot_rows[:atoms]
            ghost_rows.append(slot_rows[atoms:])
        for side in range(2):
            part = [rows_[side * ghosts : (side + 1) * ghosts] for rows_ in ghost_rows]
            ghost_out[q, side, :, :width] = jnp.concatenate(part[:2], axis=0).astype(BF16)
            ghost_out[q, side, :, width:] = jnp.concatenate(
                [part[2][:, :half_width], part[2][:, half_width:]], axis=0
            ).astype(BF16)
        if q == 0:
            pl.semaphore_wait(barrier, len(greeted))
        for side in range(2):
            ghost_copy(side, q).start()

    def span(q, part):
        start, stop = q * width, (q + 1) * width
        middle = start + half_width
        if q == CHUNKS - 1:
            stop = stop + 128
        if part == 0:
            stop = middle
        elif part == 1:
            start = middle
        return pl.ds(start, stop - start)

    slot_right = ((x + 1) % XS) * 2
    slot_left = ((x + XS - 1) % XS) * 2
    slot_far = ((x + 2) % XS) * 2

    def x_copy(kind, q):
        slot, part, to = (
            (my_slot, None, sibling),
            (my_slot, None, right),
            (my_slot, None, left),
            (slot_left + core, None, sibling),
            (slot_right + core, None, sibling),
            (slot_left + core, 0, right),
            (slot_right + core, 1, left),
            (slot_far + core, 0, sibling),
            (slot_far + core, 1, sibling),
        )[kind]
        piece = rows.at[slot, :, span(q, part)]
        if kind in (1, 2, 5, 6):
            recv = x_recv.at[(1, 2, 5, 6).index(kind), q]
        else:
            recv = sib_recv.at[0]
        return remote(piece, piece, x_send.at[0], recv, to)

    def design_of(q):
        columns = pl.ds(q * width, width)
        landed(ghost_in.at[q], ghost_recv.at[q])
        placed_rows = jnp.dot(placed, ghost_in[q], preferred_element_type=F32)
        for comp in range(3):
            if comp < 2:
                added = placed_rows[comp * atoms : (comp + 1) * atoms, :width]
            else:
                added = jnp.concatenate(
                    [placed_rows[:atoms, width:], placed_rows[atoms:, width:]], axis=1
                )
            rows[my_slot, comp * atoms : (comp + 1) * atoms, columns] = (
                (own[comp, :, columns] + added) * scale
            ).astype(BF16)
        for kind in (1, 2, 0):
            x_copy(kind, q).start()

    for q in range(CHUNKS):
        slots_of(q)
    for q in range(CHUNKS):
        design_of(q)

    for q in range(CHUNKS):
        for kind, relays in ((1, (5, 3)), (2, (6, 4))):
            x_copy(kind, q).wait_recv()
            for relay in relays:
                x_copy(relay, q).start()
    for q in range(CHUNKS):
        for kind, relay in ((5, 7), (6, 8)):
            x_copy(kind, q).wait_recv()
            x_copy(relay, q).start()
    landed(rows.at[pl.ds(0, 4)], sib_recv.at[0])

    contract = (((0,), (0,)), ((), ()))
    depth = rows.shape[0] * rows.shape[1]

    def right_block(c):
        start = pl.multiple_of(xh * half_basis + (2 * c + core) * 128, 128)
        return rows[:, :, pl.ds(start, 128)].reshape(depth, 128)

    def left_block(h, r):
        start = pl.multiple_of(xl * half_basis + (2 * r + h) * 128, 128)
        return rows[:, :, pl.ds(start, 128)].reshape(depth, 128)

    def product(by):
        r = (y + by + RING) % RING
        right_blocks = jnp.concatenate(
            [right_block((r + offset) % RING) for offset in OFFSETS], axis=1
        )
        tile = lax.dot_general(
            left_block(0, r), right_blocks, contract, preferred_element_type=F32
        )
        for k in range(BLOCKS):
            partial[0, r, k] = tile[:, k * 128 : (k + 1) * 128]
        c = (z + by + RING) % RING
        left_blocks = jnp.concatenate(
            [left_block(1, (c + RING - offset) % RING) for offset in OFFSETS], axis=1
        )
        tile = lax.dot_general(
            right_block(c), left_blocks, contract, preferred_element_type=F32
        )
        for k in range(BLOCKS):
            partial[1, c, k] = tile[:, k * 128 : (k + 1) * 128]

    ring_to = (
        (device(x, (y + 1) % RING, z, core), device(x, (y + RING - 1) % RING, z, core)),
        (device(x, y, (z + 1) % RING, core), device(x, y, (z + RING - 1) % RING, core)),
    )

    def rhs_copy_z(way, step):
        return remote(
            rhs_ring_out.at[way] if step == 0 else rhs_ring_in.at[way, step - 1],
            rhs_ring_in.at[way, step],
            rhs_send.at[0],
            rhs_ring_recv.at[way, step],
            ring_to[1][way],
        )

    def rhs_copy_y(step):
        return remote(
            rhs_mid,
            rhs_in_y.at[step - 1],
            rhs_send.at[1],
            rhs_recv.at[0],
            device(x, (y + step) % RING, z, core),
        )

    def ring_copy(h, way, step, k):
        src = ring_out.at[h, way, k] if step == 0 else ring_in.at[h, way, step - 1, k]
        return remote(
            src,
            ring_in.at[h, way, step, k],
            ring_send.at[step],
            ring_recv.at[step, k],
            ring_to[h][way],
        )

    def rhs_term(by):
        target_rows = rows[:, :, basis:].reshape(depth, 128)[:, :16]
        c = (z + by + RING) % RING
        return lax.dot_general(
            target_rows, right_block(c), contract, preferred_element_type=F32
        )[:8]

    def rhs_step(step):
        for way, length in enumerate(RHS_HOPS):
            if step >= length:
                continue
            term = rhs_term(length - step if way == 0 else step - length)
            if step == 0:
                rhs_ring_out[way] = term
            else:
                landed(rhs_ring_in.at[way, step - 1], rhs_ring_recv.at[way, step - 1])
                rhs_ring_in[way, step - 1] = rhs_ring_in[way, step - 1] + term
            rhs_copy_z(way, step).start()

    def ring_step(step, group):
        for k in ORDER[group]:
            if step > 0:
                landed(ring_in.at[:, :, step - 1, k], ring_recv.at[step - 1, k])
            for way in range(2):
                length = chain_lengths(k)[way]
                if step >= length:
                    continue
                for h in range(2):
                    here = y if h == 0 else z
                    if way == 0:
                        dest = (here + length - step) % RING
                    else:
                        dest = (here + RING - length + step) % RING
                    term = partial[h, dest, k]
                    if step == 0:
                        ring_out[h, way, k] = term.astype(BF16)
                    else:
                        ring_in[h, way, step - 1, k] = (
                            ring_in[h, way, step - 1, k].astype(F32) + term
                        ).astype(BF16)
                    ring_copy(h, way, step, k).start()

    product(4)
    product(-3)
    ring_step(0, 0)
    product(3)
    ring_step(0, 1)
    product(-2)
    ring_step(1, 0)
    product(2)
    ring_step(1, 1)
    rhs_step(0)
    product(-1)
    ring_step(2, 0)
    product(1)
    rhs_step(1)
    ring_step(2, 1)
    product(0)
    gone(ghost_out, ghost_send.at[0])
    gone(rows.at[pl.ds(0, 7)], x_send.at[0])
    rhs_step(2)
    ring_step(3, 0)
    rhs_mid[...] = rhs_term(0)
    rhs_step(3)
    ring_step(3, 1)

    def second_copy(h, k):
        if h == 0:
            to_z = (y + OFFSETS[k]) % RING
            offset = (to_z + RING - z) % RING
            to = device(x, y, to_z, core)
        else:
            to_y = (z + RING - OFFSETS[k]) % RING
            offset = (to_y + RING - y) % RING
            to = device(x, to_y, z, core)
        return remote(
            second_out.at[h, k],
            second_in.at[h, offset],
            second_send.at[k % 2],
            second_recv.at[h],
            to,
        )

    def finish(group):
        for k in ORDER[group]:
            lengths = chain_lengths(k)
            longer = lengths.index(4)
            landed(ring_in.at[:, longer, 3, k], ring_recv.at[3, k])
            for h in range(2):
                here = y if h == 0 else z
                total = partial[h, here, k]
                for way in range(2):
                    total = total + ring_in[h, way, lengths[way] - 1, k].astype(F32)

                @pl.when(delta == OFFSETS[k])
                def _():
                    kept[h] = total

                @pl.when(delta != OFFSETS[k])
                def _():
                    second_out[h, k] = total.astype(BF16)
                    second_copy(h, k).start()


    finish(0)
    for way, length in enumerate(RHS_HOPS):
        landed(rhs_ring_in.at[way, length - 1], rhs_ring_recv.at[way, length - 1])
        rhs_mid[...] += rhs_ring_in[way, length - 1]
    for to in range(1, RING):
        rhs_copy_y(to).start()

    @pl.when(sends_mirror)
    def _():
        gone(second_out.at[:, pl.ds(0, 2)], second_send.at[0])

    @pl.when(jnp.logical_not(sends_mirror))
    def _():
        gone(second_out.at[:, pl.ds(0, 3)], second_send.at[0])

    finish(1)

    def mirror_copy(h):
        return remote(
            mirror_out.at[h],
            mirror_in.at[core],
            mirror_send.at[0],
            mirror_recv.at[0],
            device(mirror_x, z, y, h),
        )

    @pl.when(jnp.logical_not(takes_mirror))
    def _():
        for h in range(2):
            total = kept[h]
            landed(second_in.at[h, pl.ds(1, RING - 1)], second_recv.at[h])
            for offset in range(1, RING):
                total = total + second_in[h, offset].astype(F32)
            flipped = total.T
            mirror_out[h] = (flipped if h == 0 else total).astype(BF16)

            @pl.when(sends_mirror)
            def _():
                mirror_copy(h).start()

            gram_ref[h * 128 : (h + 1) * 128, :] = total if h == 0 else flipped

    for step in range(3):
        gone(ring_in.at[:, :, step], ring_send.at[step])
    gone(ring_out.at[0], ring_send.at[3])

    gone(rhs_in_y, rhs_send.at[0])

    @pl.when(delta % 4 == 0)
    def _():
        gone(second_out.at[:, pl.ds(0, 1)], second_send.at[1])

    @pl.when(delta % 4 != 0)
    def _():
        gone(second_out.at[:, pl.ds(0, 2)], second_send.at[1])

    @pl.when(takes_mirror)
    def _():
        landed(mirror_in, mirror_recv.at[0])
        for sender in range(2):
            gram_ref[sender * 128 : (sender + 1) * 128, :] = mirror_in[sender].astype(F32)

    landed(rhs_in_y, rhs_recv.at[0])
    total = rhs_mid[...]
    for back in range(1, RING):
        total = total + rhs_in_y[back - 1]
    gram_ref[256:264] = total
    gone(rhs_in_y, rhs_send.at[1])

    @pl.when(sends_mirror)
    def _():
        gone(mirror_out, mirror_send.at[0])


def per_device(pair_blocks, pair_target, ghost_source, weight_code, ref_forces):
    _, pair_count, comps, basis = pair_blocks.shape
    atoms = weight_code.shape[1]
    width = basis // CHUNKS
    dom_count = lax.axis_size("dom")
    grp_count = lax.axis_size("grp")
    factor = 1.0 / math.sqrt(comps * atoms * dom_count * grp_count)
    dma = pltpu.SemaphoreType.DMA
    vmem = pl.BlockSpec(memory_space=pltpu.VMEM)
    (both,) = pl.pallas_call(
        kernel,
        out_shape=(
            jax.ShapeDtypeStruct((264, 128), F32),
        ),
        in_specs=[
            pl.BlockSpec(memory_space=pl.ANY),
        ]
        * 5,
        out_specs=(vmem,),
        scratch_shapes=[
            pltpu.VMEM((1, pair_count), jnp.int32),
            pltpu.SMEM((2, atoms // 2), jnp.int32),
            pltpu.VMEM((1, atoms), jnp.int32),
            pltpu.VMEM((comps, 1, atoms), F32),
            pltpu.VMEM((comps, pair_count, basis), BF16),
            pltpu.VMEM((comps, atoms, basis), F32),
            pltpu.VMEM((CHUNKS, 2, 16, width * 3 // 2), BF16),
            pltpu.VMEM((CHUNKS, 32, width * 3 // 2), BF16),
            pltpu.VMEM((2 * XS, comps * atoms, basis + 128), BF16),
            pltpu.VMEM((2, RING, BLOCKS, 128, 128), F32),
            pltpu.VMEM((2, 2, BLOCKS, 128, 128), BF16),
            pltpu.VMEM((2, 2, 4, BLOCKS, 128, 128), BF16),
            pltpu.VMEM((2, 128, 128), F32),
            pltpu.VMEM((2, BLOCKS, 128, 128), BF16),
            pltpu.VMEM((2, RING, 128, 128), BF16),
            pltpu.VMEM((2, 128, 128), BF16),
            pltpu.VMEM((2, 128, 128), BF16),
            pltpu.VMEM((2, 8, 128), F32),
            pltpu.VMEM((2, 4, 8, 128), F32),
            pltpu.VMEM((8, 128), F32),
            pltpu.VMEM((RING - 1, 8, 128), F32),
            dma((CHUNKS,)),
            dma((4,)),
            dma((1,)),
            dma((CHUNKS,)),
            dma((1,)),
            dma((4, CHUNKS)),
            dma((1,)),
            dma((4,)),
            dma((4, BLOCKS)),
            dma((2,)),
            dma((2,)),
            dma((1,)),
            dma((1,)),
            dma((2,)),
            dma((2, 4)),
            dma((1,)),
        ],
        compiler_params=pltpu.CompilerParams(
            collective_id=0,
            has_side_effects=True,
            vmem_limit_bytes=60 * 1024 * 1024,
        ),
    )(
        jnp.transpose(pair_blocks[0], (1, 0, 2)),
        pair_target,
        ghost_source[0, 0],
        weight_code,
        jnp.transpose(ref_forces, (2, 0, 1)),
    )
    both = both * factor
    return both[:256], both[256]


def solution(mesh):
    return jax.shard_map(
        per_device,
        mesh=mesh,
        in_specs=(
            P("grp", "dom", None, None),
            P("grp", "dom"),
            P("grp", "dom", None, None),
            P("grp", "dom"),
            P("grp", "dom", None),
        ),
        out_specs=(P("grp", "dom"), P("dom")),
        check_vma=False,
    )
```

```python
import functools
import math

import jax
import jax.numpy as jnp
from jax import lax
from jax.experimental import pallas as pl
from jax.experimental.pallas import tpu as pltpu
from jax.sharding import PartitionSpec as P

MESH = pl.DeviceIdType.MESH
RING = 8
XS = 4
OFFSETS = (6, 0, 3, 4, 1)
MIRRORED = (1, 3, 6)
BLOCKS = len(OFFSETS)
ORDER = ((0, 2, 4), (1, 3))
RHS_HOPS = (4, 3)
CHUNKS = 4
F32 = jnp.float32
BF16 = jnp.bfloat16


def chain_lengths(k):
    return (4, 3) if k % 2 == 0 else (3, 4)


def kernel(
    blocks,
    target_hbm,
    ghost_hbm,
    weight_hbm,
    force_hbm,
    gram_ref,
    target_ref,
    ghost_ref,
    weight_ref,
    force_ref,
    pairs,
    own,
    ghost_out,
    ghost_in,
    rows,
    partial,
    ring_out,
    ring_in,
    kept,
    second_out,
    second_in,
    mirror_out,
    mirror_in,
    rhs_ring_out,
    rhs_ring_in,
    rhs_mid,
    rhs_in_y,
    load_sem,
    small_sem,
    ghost_send,
    ghost_recv,
    x_send,
    x_recv,
    sib_recv,
    ring_send,
    ring_recv,
    second_send,
    second_recv,
    mirror_send,
    mirror_recv,
    rhs_send,
    rhs_ring_recv,
    rhs_recv,
):
    basis = blocks.shape[2]
    pair_count = blocks.shape[1]
    atoms = weight_ref.shape[1]
    half_basis = basis // 2
    width = basis // CHUNKS
    half_width = width // 2

    g = lax.axis_index("grp")
    d = lax.axis_index("dom")
    xl, y = g // RING, g % RING
    xh, z, core = d // (2 * RING), (d // 2) % RING, d % 2
    x = xh * 2 + xl
    delta = (z - y + RING) % RING

    def device(x_, y_, z_, core_):
        return {
            "grp": (x_ % 2) * RING + y_,
            "dom": (x_ // 2) * (2 * RING) + z_ * 2 + core_,
        }

    sibling = device(x, y, z, 1 - core)
    right = device((x + 1) % XS, y, z, core)
    left = device((x + XS - 1) % XS, y, z, core)
    dom_count = 4 * RING
    below = {"grp": g, "dom": (d + dom_count - 1) % dom_count}
    above = {"grp": g, "dom": (d + 1) % dom_count}
    off_chip = {"grp": g, "dom": (d + dom_count - 1 + 2 * core) % dom_count}
    mirror_x = (x % 2) * 2 + x // 2

    def remote(src, dst, send_sem, recv_sem, to):
        return pltpu.make_async_remote_copy(
            src_ref=src,
            dst_ref=dst,
            send_sem=send_sem,
            recv_sem=recv_sem,
            device_id=to,
            device_id_type=MESH,
        )

    def landed(ref, sem):
        remote(ref, ref, sem, sem, sibling).wait_recv()

    def gone(ref, sem):
        remote(ref, ref, sem, sem, sibling).wait_send()

    def load(q):
        columns = pl.ds(q * width, width)
        return pltpu.make_async_copy(
            blocks.at[:, :, columns], pairs.at[:, :, columns], load_sem.at[q]
        )

    small_loads = [
        pltpu.make_async_copy(source, place, small_sem.at[i])
        for i, (source, place) in enumerate(
            (
                (target_hbm, target_ref),
                (ghost_hbm, ghost_ref),
                (weight_hbm, weight_ref),
                (force_hbm, force_ref),
            )
        )
    ]
    for copy in small_loads:
        copy.start()
    for q in range(CHUNKS):
        load(q).start()

    barrier = pltpu.get_barrier_semaphore()

    def greet(to):
        pl.semaphore_signal(barrier, inc=1, device_id=to, device_id_type=MESH)

    up, down = (device(x, (y + by) % RING, z, core) for by in (1, RING - 1))
    greeted = (off_chip, sibling, right, left, up, down)
    for to in greeted:
        greet(to)

    sends_mirror = (delta == MIRRORED[0]) | (delta == MIRRORED[1]) | (delta == MIRRORED[2])
    takes_mirror = jnp.logical_not(sends_mirror) & (delta % 4 != 0)

    for copy in small_loads:
        copy.wait()

    slots = 2 * atoms
    per_atom = pair_count // atoms
    slot_ids = lax.broadcasted_iota(jnp.int32, (slots, pair_count), 0)
    pair_ids = lax.broadcasted_iota(jnp.int32, (slots, pair_count), 1)
    center = pair_ids // per_atom
    signs = (
        (slot_ids == center).astype(F32) - (slot_ids == target_ref[...]).astype(F32)
    ).astype(BF16)

    ghosts = atoms // 2
    row_ids = lax.broadcasted_iota(jnp.int32, (2 * atoms, 2 * atoms), 0)
    col_ids = lax.broadcasted_iota(jnp.int32, (2 * atoms, 2 * atoms), 1)
    source = jnp.zeros((2 * atoms, 2 * atoms), jnp.int32)
    for side in range(2):
        for ghost in range(ghosts):
            here = (col_ids // atoms == side) & (col_ids % ghosts == ghost)
            source = jnp.where(here, ghost_ref[side, ghost], source)
    placed = (row_ids % atoms == source) & (
        row_ids // atoms == (col_ids // ghosts) % 2
    )
    placed = placed.astype(F32).astype(BF16)

    diagonal = lax.broadcasted_iota(jnp.int32, (atoms, atoms), 0) == (
        lax.broadcasted_iota(jnp.int32, (atoms, atoms), 1)
    )

    def as_column(row):
        return jnp.sum(jnp.where(diagonal, row, 0.0), axis=1, keepdims=True)

    scale = as_column((1.0 + weight_ref[...].astype(F32)) * 0.5)
    first_lane = lax.broadcasted_iota(jnp.int32, (atoms, 128), 1) == 0
    my_slot = x * 2 + core
    for comp in range(3):
        column = as_column(force_ref[comp]) * scale
        rows[my_slot, comp * atoms : (comp + 1) * atoms, basis:] = jnp.where(
            first_lane, column, 0.0
        ).astype(BF16)

    def ghost_copy(side, q):
        return remote(
            ghost_out.at[q, side],
            ghost_in.at[q, pl.ds(side * 16, 16)],
            ghost_send.at[0],
            ghost_recv.at[q],
            below if side == 0 else above,
        )

    def slots_of(q):
        load(q).wait()
        columns = pl.ds(q * width, width)
        ghost_rows = []
        for comp in range(3):
            slot_rows = jnp.dot(signs, pairs[comp, :, columns], preferred_element_type=F32)
            own[comp, :, columns] = slot_rows[:atoms]
            ghost_rows.append(slot_rows[atoms:])
        for side in range(2):
            part = [rows_[side * ghosts : (side + 1) * ghosts] for rows_ in ghost_rows]
            ghost_out[q, side, :, :width] = jnp.concatenate(part[:2], axis=0).astype(BF16)
            ghost_out[q, side, :, width:] = jnp.concatenate(
                [part[2][:, :half_width], part[2][:, half_width:]], axis=0
            ).astype(BF16)
        if q == 0:
            pl.semaphore_wait(barrier, len(greeted))
        for side in range(2):
            ghost_copy(side, q).start()

    def span(q, part):
        start, stop = q * width, (q + 1) * width
        middle = start + half_width
        if q == CHUNKS - 1:
            stop = stop + 128
        if part == 0:
            stop = middle
        elif part == 1:
            start = middle
        return pl.ds(start, stop - start)

    slot_right = ((x + 1) % XS) * 2
    slot_left = ((x + XS - 1) % XS) * 2
    slot_far = ((x + 2) % XS) * 2

    def x_copy(kind, q):
        slot, part, to = (
            (my_slot, None, sibling),
            (my_slot, None, right),
            (my_slot, None, left),
            (slot_left + core, None, sibling),
            (slot_right + core, None, sibling),
            (slot_left + core, 0, right),
            (slot_right + core, 1, left),
            (slot_far + core, 0, sibling),
            (slot_far + core, 1, sibling),
        )[kind]
        piece = rows.at[slot, :, span(q, part)]
        if kind in (1, 2, 5, 6):
            recv = x_recv.at[(1, 2, 5, 6).index(kind), q]
        else:
            recv = sib_recv.at[0]
        return remote(piece, piece, x_send.at[0], recv, to)

    def design_of(q):
        columns = pl.ds(q * width, width)
        landed(ghost_in.at[q], ghost_recv.at[q])
        placed_rows = jnp.dot(placed, ghost_in[q], preferred_element_type=F32)
        for comp in range(3):
            if comp < 2:
                added = placed_rows[comp * atoms : (comp + 1) * atoms, :width]
            else:
                added = jnp.concatenate(
                    [placed_rows[:atoms, width:], placed_rows[atoms:, width:]], axis=1
                )
            rows[my_slot, comp * atoms : (comp + 1) * atoms, columns] = (
                (own[comp, :, columns] + added) * scale
            ).astype(BF16)
        for kind in (1, 2, 0):
            x_copy(kind, q).start()

    for q in range(CHUNKS):
        slots_of(q)
    for q in range(CHUNKS):
        design_of(q)

    for q in range(CHUNKS):
        for kind, relays in ((1, (5, 3)), (2, (6, 4))):
            x_copy(kind, q).wait_recv()
            for relay in relays:
                x_copy(relay, q).start()
    for q in range(CHUNKS):
        for kind, relay in ((5, 7), (6, 8)):
            x_copy(kind, q).wait_recv()
            x_copy(relay, q).start()
    landed(rows.at[pl.ds(0, 4)], sib_recv.at[0])

    contract = (((0,), (0,)), ((), ()))
    depth = rows.shape[0] * rows.shape[1]

    def right_block(c):
        start = pl.multiple_of(xh * half_basis + (2 * c + core) * 128, 128)
        return rows[:, :, pl.ds(start, 128)].reshape(depth, 128)

    def left_block(h, r):
        start = pl.multiple_of(xl * half_basis + (2 * r + h) * 128, 128)
        return rows[:, :, pl.ds(start, 128)].reshape(depth, 128)

    def product(by):
        r = (y + by + RING) % RING
        right_blocks = jnp.concatenate(
            [right_block((r + offset) % RING) for offset in OFFSETS], axis=1
        )
        tile = lax.dot_general(
            left_block(0, r), right_blocks, contract, preferred_element_type=F32
        )
        for k in range(BLOCKS):
            partial[0, r, k] = tile[:, k * 128 : (k + 1) * 128]
        c = (z + by + RING) % RING
        left_blocks = jnp.concatenate(
            [left_block(1, (c + RING - offset) % RING) for offset in OFFSETS], axis=1
        )
        tile = lax.dot_general(
            right_block(c), left_blocks, contract, preferred_element_type=F32
        )
        for k in range(BLOCKS):
            partial[1, c, k] = tile[:, k * 128 : (k + 1) * 128]

    ring_to = (
        (device(x, (y + 1) % RING, z, core), device(x, (y + RING - 1) % RING, z, core)),
        (device(x, y, (z + 1) % RING, core), device(x, y, (z + RING - 1) % RING, core)),
    )

    def rhs_copy_z(way, step):
        return remote(
            rhs_ring_out.at[way] if step == 0 else rhs_ring_in.at[way, step - 1],
            rhs_ring_in.at[way, step],
            rhs_send.at[0],
            rhs_ring_recv.at[way, step],
            ring_to[1][way],
        )

    def rhs_copy_y(step):
        return remote(
            rhs_mid,
            rhs_in_y.at[step - 1],
            rhs_send.at[1],
            rhs_recv.at[0],
            device(x, (y + step) % RING, z, core),
        )

    def ring_copy(h, way, step, k):
        src = ring_out.at[h, way, k] if step == 0 else ring_in.at[h, way, step - 1, k]
        return remote(
            src,
            ring_in.at[h, way, step, k],
            ring_send.at[step],
            ring_recv.at[step, k],
            ring_to[h][way],
        )

    def rhs_term(by):
        target_rows = rows[:, :, basis:].reshape(depth, 128)[:, :16]
        c = (z + by + RING) % RING
        return lax.dot_general(
            target_rows, right_block(c), contract, preferred_element_type=F32
        )[:8]

    def rhs_step(step):
        for way, length in enumerate(RHS_HOPS):
            if step >= length:
                continue
            term = rhs_term(length - step if way == 0 else step - length)
            if step == 0:
                rhs_ring_out[way] = term
            else:
                landed(rhs_ring_in.at[way, step - 1], rhs_ring_recv.at[way, step - 1])
                rhs_ring_in[way, step - 1] = rhs_ring_in[way, step - 1] + term
            rhs_copy_z(way, step).start()

    def ring_step(step, group):
        for k in ORDER[group]:
            if step > 0:
                landed(ring_in.at[:, :, step - 1, k], ring_recv.at[step - 1, k])
            for way in range(2):
                length = chain_lengths(k)[way]
                if step >= length:
                    continue
                for h in range(2):
                    here = y if h == 0 else z
                    if way == 0:
                        dest = (here + length - step) % RING
                    else:
                        dest = (here + RING - length + step) % RING
                    term = partial[h, dest, k]
                    if step == 0:
                        ring_out[h, way, k] = term.astype(BF16)
                    else:
                        ring_in[h, way, step - 1, k] = (
                            ring_in[h, way, step - 1, k].astype(F32) + term
                        ).astype(BF16)
                    ring_copy(h, way, step, k).start()

    product(4)
    product(-3)
    ring_step(0, 0)
    product(3)
    ring_step(0, 1)
    rhs_step(0)
    product(-2)
    ring_step(1, 0)
    product(2)
    ring_step(1, 1)
    rhs_step(1)
    product(-1)
    ring_step(2, 0)
    product(1)
    ring_step(2, 1)
    rhs_step(2)
    product(0)
    gone(ghost_out, ghost_send.at[0])
    gone(rows.at[pl.ds(0, 7)], x_send.at[0])
    rhs_mid[...] = rhs_term(0)
    ring_step(3, 0)
    ring_step(3, 1)
    rhs_step(3)

    def second_copy(h, k):
        if h == 0:
            to_z = (y + OFFSETS[k]) % RING
            offset = (to_z + RING - z) % RING
            to = device(x, y, to_z, core)
        else:
            to_y = (z + RING - OFFSETS[k]) % RING
            offset = (to_y + RING - y) % RING
            to = device(x, to_y, z, core)
        return remote(
            second_out.at[h, k],
            second_in.at[h, offset],
            second_send.at[k % 2],
            second_recv.at[h],
            to,
        )

    def finish(group):
        for k in ORDER[group]:
            lengths = chain_lengths(k)
            longer = lengths.index(4)
            landed(ring_in.at[:, longer, 3, k], ring_recv.at[3, k])
            for h in range(2):
                here = y if h == 0 else z
                total = partial[h, here, k]
                for way in range(2):
                    total = total + ring_in[h, way, lengths[way] - 1, k].astype(F32)

                @pl.when(delta == OFFSETS[k])
                def _():
                    kept[h] = total

                @pl.when(delta != OFFSETS[k])
                def _():
                    second_out[h, k] = total.astype(BF16)
                    second_copy(h, k).start()


    finish(0)
    for way, length in enumerate(RHS_HOPS):
        landed(rhs_ring_in.at[way, length - 1], rhs_ring_recv.at[way, length - 1])
        rhs_mid[...] += rhs_ring_in[way, length - 1]
    for to in range(1, RING):
        rhs_copy_y(to).start()

    @pl.when(sends_mirror)
    def _():
        gone(second_out.at[:, pl.ds(0, 2)], second_send.at[0])

    @pl.when(jnp.logical_not(sends_mirror))
    def _():
        gone(second_out.at[:, pl.ds(0, 3)], second_send.at[0])

    finish(1)

    def mirror_copy(h):
        return remote(
            mirror_out.at[h],
            mirror_in.at[core],
            mirror_send.at[0],
            mirror_recv.at[0],
            device(mirror_x, z, y, h),
        )

    @pl.when(jnp.logical_not(takes_mirror))
    def _():
        for h in range(2):
            total = kept[h]
            landed(second_in.at[h, pl.ds(1, RING - 1)], second_recv.at[h])
            for offset in range(1, RING):
                total = total + second_in[h, offset].astype(F32)
            flipped = total.T
            mirror_out[h] = (flipped if h == 0 else total).astype(BF16)

            @pl.when(sends_mirror)
            def _():
                mirror_copy(h).start()

            gram_ref[h * 128 : (h + 1) * 128, :] = total if h == 0 else flipped

    for step in range(3):
        gone(ring_in.at[:, :, step], ring_send.at[step])
    gone(ring_out.at[0], ring_send.at[3])

    gone(rhs_in_y, rhs_send.at[0])

    @pl.when(delta % 4 == 0)
    def _():
        gone(second_out.at[:, pl.ds(0, 1)], second_send.at[1])

    @pl.when(delta % 4 != 0)
    def _():
        gone(second_out.at[:, pl.ds(0, 2)], second_send.at[1])

    @pl.when(takes_mirror)
    def _():
        landed(mirror_in, mirror_recv.at[0])
        for sender in range(2):
            gram_ref[sender * 128 : (sender + 1) * 128, :] = mirror_in[sender].astype(F32)

    landed(rhs_in_y, rhs_recv.at[0])
    total = rhs_mid[...]
    for back in range(1, RING):
        total = total + rhs_in_y[back - 1]
    gram_ref[256:264] = total
    gone(rhs_in_y, rhs_send.at[1])

    @pl.when(sends_mirror)
    def _():
        gone(mirror_out, mirror_send.at[0])


def per_device(pair_blocks, pair_target, ghost_source, weight_code, ref_forces):
    _, pair_count, comps, basis = pair_blocks.shape
    atoms = weight_code.shape[1]
    width = basis // CHUNKS
    dom_count = lax.axis_size("dom")
    grp_count = lax.axis_size("grp")
    factor = 1.0 / math.sqrt(comps * atoms * dom_count * grp_count)
    dma = pltpu.SemaphoreType.DMA
    vmem = pl.BlockSpec(memory_space=pltpu.VMEM)
    (both,) = pl.pallas_call(
        kernel,
        out_shape=(
            jax.ShapeDtypeStruct((264, 128), F32),
        ),
        in_specs=[
            pl.BlockSpec(memory_space=pl.ANY),
        ]
        * 5,
        out_specs=(vmem,),
        scratch_shapes=[
            pltpu.VMEM((1, pair_count), jnp.int32),
            pltpu.SMEM((2, atoms // 2), jnp.int32),
            pltpu.VMEM((1, atoms), jnp.int32),
            pltpu.VMEM((comps, 1, atoms), F32),
            pltpu.VMEM((comps, pair_count, basis), BF16),
            pltpu.VMEM((comps, atoms, basis), F32),
            pltpu.VMEM((CHUNKS, 2, 16, width * 3 // 2), BF16),
            pltpu.VMEM((CHUNKS, 32, width * 3 // 2), BF16),
            pltpu.VMEM((2 * XS, comps * atoms, basis + 128), BF16),
            pltpu.VMEM((2, RING, BLOCKS, 128, 128), F32),
            pltpu.VMEM((2, 2, BLOCKS, 128, 128), BF16),
            pltpu.VMEM((2, 2, 4, BLOCKS, 128, 128), BF16),
            pltpu.VMEM((2, 128, 128), F32),
            pltpu.VMEM((2, BLOCKS, 128, 128), BF16),
            pltpu.VMEM((2, RING, 128, 128), BF16),
            pltpu.VMEM((2, 128, 128), BF16),
            pltpu.VMEM((2, 128, 128), BF16),
            pltpu.VMEM((2, 8, 128), F32),
            pltpu.VMEM((2, 4, 8, 128), F32),
            pltpu.VMEM((8, 128), F32),
            pltpu.VMEM((RING - 1, 8, 128), F32),
            dma((CHUNKS,)),
            dma((4,)),
            dma((1,)),
            dma((CHUNKS,)),
            dma((1,)),
            dma((4, CHUNKS)),
            dma((1,)),
            dma((4,)),
            dma((4, BLOCKS)),
            dma((2,)),
            dma((2,)),
            dma((1,)),
            dma((1,)),
            dma((2,)),
            dma((2, 4)),
            dma((1,)),
        ],
        compiler_params=pltpu.CompilerParams(
            collective_id=0,
            has_side_effects=True,
            vmem_limit_bytes=60 * 1024 * 1024,
        ),
    )(
        jnp.transpose(pair_blocks[0], (1, 0, 2)),
        pair_target,
        ghost_source[0, 0],
        weight_code,
        jnp.transpose(ref_forces, (2, 0, 1)),
    )
    both = both * factor
    return both[:256], both[256]


def solution(mesh):
    return jax.shard_map(
        per_device,
        mesh=mesh,
        in_specs=(
            P("grp", "dom", None, None),
            P("grp", "dom"),
            P("grp", "dom", None, None),
            P("grp", "dom"),
            P("grp", "dom", None),
        ),
        out_specs=(P("grp", "dom"), P("dom")),
        check_vma=False,
    )
```
